32 devices in a mesh: lat: 8 (over z, x), lev: 4 (over y, core).
Axes of the slice: x: 2, y: 2, z: 4, core: 2. Of those that a mesh axis runs over, the one named last changes fastest.
Arguments:
- particle_mass_fraction: float32 [20, 64, 8, 360], P(None, 'lat', 'lev'), may hold values from 0.1 to 2
- meridional_cfl_factor: float32 [64, 8, 360], P('lat', 'lev'), may hold values from -0.45 to 0.45
- thermal_state_kelvins: float32 [64, 8, 360], P('lat', 'lev'), may hold values from 200 to 300
- logarithmic_barometric_span: float32 [8], P('lev'), may hold values from 0.06 to 0.2
- gravitational_fall_kilometres: float32 [20], replicated, may hold values from 0.02 to 20
- zonal_cfl_factor: float32 [64, 8, 360], P('lat', None, 'lev'), may hold values from -0.45 to 0.45
- collision_rate_matrix: float32 [20, 20], replicated, may hold values from 0.02 to 0.2
Outputs:
- dust_out: float32 [20, 64, 8, 360], P(None, 'lat', None, 'lev')
- height: float32 [64, 8, 360], P('lat', 'lev')
The draws below stay inside these ranges and needn't reach their ends.
All inputs are finite; a program needn't handle non-finite values.
Results may differ from the reference program's by a relative error of at most 0.000067.
Values sent between devices are 32-bit elements; how exact they have to be, the bound alone decides.
A program may use at most 128 MiB of HBM per device.

```python
import math
import jax
import jax.numpy as jnp
from jax import lax

BINS = 20
MERIDIAN_POINTS = 64
VERTICAL_TIERS = 8
ZONAL_POINTS = 360


def level_of(own_key, extent, cuts, low, largest):
    loudness, own = 1.0, jax.random.fold_in(own_key, 6)
    for dim, shards_of in cuts:
        heights = jnp.exp(jax.random.uniform(jax.random.fold_in(own, dim), (shards_of,), jnp.float32, low / len(cuts), largest / len(cuts)))
        loudness = loudness * jnp.repeat(heights, extent[dim] // shards_of).reshape([-1 if axis == dim else 1 for axis in range(len(extent))])
    return loudness


def setup_inputs(seed: int = 0) -> dict:
    keys = jax.random.split(jax.random.key(seed), 8)
    particle_mass_fraction = jnp.clip(jnp.exp(math.log(2.0) - 2.9957323 * jax.random.uniform(keys[0], (BINS, MERIDIAN_POINTS, VERTICAL_TIERS, ZONAL_POINTS), jnp.float32) ** level_of(keys[0], (BINS, MERIDIAN_POINTS, VERTICAL_TIERS, ZONAL_POINTS), ((1, 8), (2, 4)), -0.2, 0.2)), 0.1, 2.0)
    meridional_cfl_factor = jnp.clip(jax.random.uniform(keys[1], (MERIDIAN_POINTS, VERTICAL_TIERS, ZONAL_POINTS), jnp.float32, -0.45, 0.45) * level_of(keys[1], (MERIDIAN_POINTS, VERTICAL_TIERS, ZONAL_POINTS), ((0, 8), (1, 4)), -0.4, 0.0), -0.45, 0.45)
    thermal_state_kelvins = jnp.clip(200.0 + 100.0 * jax.random.uniform(keys[2], (MERIDIAN_POINTS, VERTICAL_TIERS, ZONAL_POINTS), jnp.float32) ** level_of(keys[2], (MERIDIAN_POINTS, VERTICAL_TIERS, ZONAL_POINTS), ((0, 8), (1, 4)), -0.2, 0.2), 200.0, 300.0)
    logarithmic_barometric_span = jnp.clip(jnp.exp(math.log(0.2) - 1.2039728 * jax.random.uniform(keys[3], (VERTICAL_TIERS,), jnp.float32) ** level_of(keys[3], (VERTICAL_TIERS,), ((0, 4),), -0.2, 0.2)), 0.06, 0.2)
    gravitational_fall_kilometres = jnp.clip(jnp.exp(jax.random.uniform(keys[4], (BINS,), jnp.float32, math.log(0.02), math.log(20.0))), 0.02, 20.0)
    zonal_cfl_factor = jnp.clip(jax.random.uniform(keys[5], (MERIDIAN_POINTS, VERTICAL_TIERS, ZONAL_POINTS), jnp.float32, -0.45, 0.45) * level_of(keys[5], (MERIDIAN_POINTS, VERTICAL_TIERS, ZONAL_POINTS), ((0, 8), (2, 4)), -0.4, 0.0), -0.45, 0.45)
    collision_rate_matrix = jnp.clip(jnp.exp(jax.random.uniform(keys[6], (BINS, BINS), jnp.float32, math.log(0.02), math.log(0.2))), 0.02, 0.2)
    return {"particle_mass_fraction": particle_mass_fraction, "meridional_cfl_factor": meridional_cfl_factor, "thermal_state_kelvins": thermal_state_kelvins, "logarithmic_barometric_span": logarithmic_barometric_span, "gravitational_fall_kilometres": gravitational_fall_kilometres, "zonal_cfl_factor": zonal_cfl_factor, "collision_rate_matrix": collision_rate_matrix}


specific_air_factor = 0.0293
scale_height = 7.0


def settle_sweep(mixing, settle_rate, inflow):
    def stepper(flux_in, inputs):
        level_mix, level_rate = inputs
        summed = level_mix + flux_in
        return level_rate / (1.0 + level_rate) * summed, summed / (1.0 + level_rate)

    _, swept = lax.scan(stepper, inflow, (jnp.moveaxis(mixing, 2, 0), jnp.moveaxis(settle_rate, 2, 0)))
    return jnp.moveaxis(swept, 0, 2)


def reference(particle_mass_fraction, meridional_cfl_factor, thermal_state_kelvins, logarithmic_barometric_span, gravitational_fall_kilometres, zonal_cfl_factor, collision_rate_matrix):
    rows_below = jnp.pad(particle_mass_fraction, ((0, 0), (1, 0), (0, 0), (0, 0)))[:, :-1]
    south_flux = jnp.maximum(meridional_cfl_factor, 0.0) * rows_below + jnp.minimum(meridional_cfl_factor, 0.0) * particle_mass_fraction
    north_flux = jnp.pad(south_flux, ((0, 0), (0, 1), (0, 0), (0, 0)))[:, 1:]
    advected = particle_mass_fraction + south_flux - north_flux
    vertical_span_height = specific_air_factor * thermal_state_kelvins * logarithmic_barometric_span[None, :, None]
    height = jnp.cumsum(vertical_span_height[:, ::-1], axis=1)[:, ::-1] - 0.5 * vertical_span_height
    density = jnp.exp(-height / scale_height)
    settle_rate = gravitational_fall_kilometres[:, None, None, None] / vertical_span_height[None]
    inflow = jnp.zeros((particle_mass_fraction.shape[0], particle_mass_fraction.shape[1], particle_mass_fraction.shape[3]), jnp.float32)
    settled = settle_sweep(advected, settle_rate, inflow)
    west_mix = jnp.roll(settled, 1, axis=3)
    west_flux = jnp.maximum(zonal_cfl_factor, 0.0) * west_mix + jnp.minimum(zonal_cfl_factor, 0.0) * settled
    east_flux = jnp.roll(west_flux, -1, axis=3)
    moved = settled + west_flux - east_flux
    merging = jnp.tril(collision_rate_matrix, -1) - jnp.triu(collision_rate_matrix, 1)
    coag_rate = jnp.einsum("bc,clkx->blkx", merging, moved, precision=lax.Precision.HIGHEST)
    return moved + density * moved * coag_rate, height
```

```python
import functools

import jax
import jax.numpy as jnp
from jax import lax
from jax.experimental import pallas as pl
from jax.experimental.pallas import tpu as pltpu
from jax.sharding import PartitionSpec as P

specific_air_factor = 0.0293
scale_height = 7.0
LANES = 128
MESH = pl.DeviceIdType.MESH
HIGHEST = lax.Precision.HIGHEST


def widen(x):
    short = -x.shape[-1] % LANES
    if short:
        x = jnp.concatenate([x, jnp.zeros((*x.shape[:-1], short), x.dtype)], -1)
    return x


def lon_block(tile, total, width, block):
    axis = 2
    count = -(-total // LANES)
    last = total % LANES
    start = block * width - 1
    c, off = start // LANES, start % LANES

    def piece(i):
        if i < 0:
            return pltpu.roll(tile(count - 1), (LANES - last) % LANES, axis)
        if i == count:
            return tile(0)
        x = tile(i)
        if i == count - 1 and last and total < start + width + 2:
            lane = lax.broadcasted_iota(jnp.int32, x.shape, axis)
            x = jnp.where(lane < last, x, pltpu.roll(tile(0), last, axis))
        return x

    x = piece(c)
    if off + width + 2 > LANES:
        lane = lax.broadcasted_iota(jnp.int32, x.shape, axis)
        x = jnp.where(lane >= off, x, piece(c + 1))
    return pltpu.roll(x, (2 * LANES - off - 1) % LANES, axis)


def spare(lane, width):
    return (lane > width) & (lane < LANES - 1)


def stow(x, d, width, p):
    free = LANES - 2 - width
    lane = lax.broadcasted_iota(jnp.int32, x.shape, 2)
    return jnp.where(spare(lane, width), pltpu.roll(d, (width + 2 - p * free) % LANES, 2), x)


def unstow(parts, width):
    free = LANES - 2 - width
    back = [pltpu.roll(x, (p * free - width - 2) % LANES, 2) for p, x in enumerate(parts)]
    lane = lax.broadcasted_iota(jnp.int32, back[0].shape, 2)
    later = jnp.where(lane < 2 * free - 1, back[1], back[2])
    return jnp.where((lane < free - 1) | (lane == LANES - 1), back[0], later)


def kernel(
    n_lat, n_lev,
    q_hbm, mc_hbm, temp_hbm, span_hbm, fall_hbm, zc_hbm, rate_hbm,
    out_ref, height_ref,
    q_ref, mc_ref, temp_ref, span_ref, fall_ref, zc_ref, rate_ref,
    main_s, main_r, thick_s, thick_r, north_s, north_r, south_s, south_r,
    tot_s, tot_r, zc_s, zc_r, inverse, advected, kron, dens,
    main_ss, main_rs, thick_ss, thick_rs, north_ss, north_rs, south_ss, south_rs,
    tot_ss, tot_rs, zc_sem, own_sem, load_sem,
):
    i, j = lax.axis_index("lat"), lax.axis_index("lev")
    loads = [
        pltpu.make_async_copy(src, dst, load_sem.at[number])
        for number, (src, dst) in enumerate((
            (span_hbm, span_ref), (temp_hbm, temp_ref), (zc_hbm, zc_ref), (mc_hbm, mc_ref),
            (q_hbm, q_ref), (fall_hbm, fall_ref), (rate_hbm, rate_ref)))
    ]
    for load in loads:
        load.start()
    bins, rows, levels, total = q_ref.shape
    width = total // n_lev
    left, right = lax.rem(j + n_lev - 1, n_lev), lax.rem(j + 1, n_lev)
    has_south, has_north = i > 0, i < n_lat - 1

    barrier = pltpu.get_barrier_semaphore()
    for d in range(1, n_lev):
        pl.semaphore_signal(barrier, inc=1, device_id=(i, lax.rem(j + d, n_lev)), device_id_type=MESH)

    @pl.when(has_south)
    def _():
        for m in range(n_lev):
            pl.semaphore_signal(barrier, inc=1, device_id=(i - 1, m), device_id_type=MESH)

    @pl.when(has_north)
    def _():
        for m in range(n_lev):
            pl.semaphore_signal(barrier, inc=1, device_id=(i + 1, m), device_id_type=MESH)

    for load in loads[:3]:
        load.wait()
    thick = [specific_air_factor * temp_ref[:, k, :] * span_ref[k] for k in range(levels)]
    tot = thick[0]
    for k in range(1, levels):
        tot = tot + thick[k]
    tot_s[...] = widen(tot)
    for m in range(n_lev):
        for k in range(levels):
            wide = widen(thick[k])[None]
            tile = lambda c: wide[:, :, c * LANES : (c + 1) * LANES]
            thick_s[m, k] = lon_block(tile, total, width, m)[0]
    zc_s[...] = widen(zc_ref[...])

    peers = n_lev - 1 + n_lev * (jnp.minimum(i, 1) + jnp.minimum(n_lat - 1 - i, 1))

    def thick_copy(m):
        return pltpu.make_async_remote_copy(
            thick_s.at[m], thick_r.at[j], thick_ss.at[m], thick_rs.at[j], (i, m), MESH)

    def main_copy(m):
        return pltpu.make_async_remote_copy(
            main_s.at[m], main_r.at[j], main_ss.at[m], main_rs.at[j], (i, m), MESH)

    def tot_copy(m):
        return pltpu.make_async_remote_copy(
            tot_s, tot_r.at[j], tot_ss.at[m], tot_rs.at[j], (i, m), MESH)

    def north_copy(m):
        return pltpu.make_async_remote_copy(
            north_s.at[m], north_r.at[j], north_ss.at[m], north_rs.at[j], (i + 1, m), MESH)

    def south_copy(m):
        return pltpu.make_async_remote_copy(
            south_s.at[m], south_r.at[j], south_ss.at[m], south_rs.at[j], (i - 1, m), MESH)

    zc_copy = pltpu.make_async_remote_copy(
        zc_s, zc_r, zc_sem.at[0], zc_sem.at[1], (i, left), MESH)

    def tile_of(ref, k):
        def tile(c):
            stop = min((c + 1) * LANES, total)
            return widen(ref[:, :, k, c * LANES : stop])
        return tile

    def mc_tile(k):
        def tile(c):
            stop = min((c + 1) * LANES, total)
            return widen(mc_ref[:, k, c * LANES : stop])[None]
        return tile

    for load in loads[3:5]:
        load.wait()
    group = bins // 4

    def cut_block(m):
        for k in range(levels):
            x = lon_block(tile_of(q_ref, k), total, width, m)
            for p in range(3):
                main_s[m, k, pl.ds(p * group, group)] = stow(
                    x[p * group : (p + 1) * group], x[3 * group :], width, p)
            main_s[m, k, pl.ds(3 * group, 1)] = lon_block(mc_tile(k), total, width, m)
            south_s[m, k] = main_s[m, k, :, 0, :]
            north_s[m, k] = main_s[m, k, :, rows - 1, :]

    def send_edges(m):
        @pl.when(has_south)
        def _():
            south_copy(m).start()

        @pl.when(has_north)
        def _():
            north_copy(m).start()

    half_way = n_lev // 2
    base = half_way * (j // half_way)

    def cut_half(first):
        for m in range(first, first + half_way):
            cut_block(m)

    @pl.when(j >= half_way)
    def _():
        cut_half(0)

    @pl.when(j < half_way)
    def _():
        cut_half(half_way)

    pl.semaphore_wait(barrier, peers)

    for m in range(n_lev):
        @pl.when(j != m)
        def _():
            thick_copy(m).start()
    for s in range(half_way):
        main_copy(half_way - base + s).start()
    for s in range(half_way):
        send_edges(half_way - base + s)
    zc_copy.start()

    @pl.when(j >= half_way)
    def _():
        cut_half(half_way)

    @pl.when(j < half_way)
    def _():
        cut_half(0)

    for s in range(half_way):
        m = base + s

        @pl.when(j != m)
        def _():
            main_copy(m).start()
        send_edges(m)

    for m in range(n_lev):
        @pl.when(j > m)
        def _():
            tot_copy(m).start()

    own = [pltpu.make_async_copy(main_s.at[j], main_r.at[j], own_sem.at[0]),
           pltpu.make_async_copy(thick_s.at[j], thick_r.at[j], own_sem.at[1])]
    for copy in own:
        copy.start()

    @pl.when(jnp.logical_not(has_south))
    def _():
        north_r[...] = jnp.zeros_like(north_r)

    @pl.when(jnp.logical_not(has_north))
    def _():
        south_r[...] = jnp.zeros_like(south_r)

    for load in loads[5:]:
        load.wait()
    rate = rate_ref[...]
    r0 = lax.broadcasted_iota(jnp.int32, rate.shape, 0)
    r1 = lax.broadcasted_iota(jnp.int32, rate.shape, 1)
    merging = jnp.where(r1 < r0, rate, jnp.where(r1 > r0, -rate, 0.0))
    cells = bins * rows
    e0 = lax.broadcasted_iota(jnp.int32, (cells, bins), 0)
    e1 = lax.broadcasted_iota(jnp.int32, (cells, bins), 1)
    spread = jnp.where((e0 >= e1 * rows) & (e0 < (e1 + 1) * rows), 1.0, 0.0)
    half = jnp.dot(spread, merging, precision=HIGHEST, preferred_element_type=jnp.float32)
    full = lax.dot_general(half, spread, (((1,), (1,)), ((), ())), precision=HIGHEST,
                           preferred_element_type=jnp.float32)
    k0 = lax.broadcasted_iota(jnp.int32, full.shape, 0)
    k1 = lax.broadcasted_iota(jnp.int32, full.shape, 1)
    kron[...] = jnp.where(lax.rem(k0, rows) == lax.rem(k1, rows), full, 0.0)

    own[1].wait()
    for m in range(n_lev):
        @pl.when(j != m)
        def _():
            pltpu.make_async_remote_copy(
                thick_s.at[m], thick_r.at[m], thick_ss.at[m], thick_rs.at[m], (i, m), MESH).wait_recv()
    below = jnp.zeros((rows, LANES), jnp.float32)
    for k in reversed(range(n_lev * levels)):
        t = thick_r[k // levels, k % levels]
        dens[k] = jnp.exp((below + 0.5 * t) * (-1.0 / scale_height))
        below = below + t
        for b in range(bins):
            inverse[k, b] = 1.0 / (t + fall_ref[b])

    own[0].wait()

    sub = lax.broadcasted_iota(jnp.int32, (1, rows, LANES), 1)
    lane = lax.broadcasted_iota(jnp.int32, (1, rows, LANES), 2)
    for s in range(n_lev):
        m = lax.rem(base + s, n_lev)

        @pl.when(j != m)
        def _():
            pltpu.make_async_remote_copy(
                main_s.at[m], main_r.at[m], main_ss.at[m], main_rs.at[m], (i, m), MESH).wait_recv()

        @pl.when(has_south)
        def _():
            pltpu.make_async_remote_copy(
                north_s.at[m], north_r.at[m], north_ss.at[m], north_rs.at[m], (i - 1, m), MESH).wait_recv()

        @pl.when(has_north)
        def _():
            pltpu.make_async_remote_copy(
                south_s.at[m], south_r.at[m], south_ss.at[m], south_rs.at[m], (i + 1, m), MESH).wait_recv()

        for kk in range(levels):
            q = main_r[m, kk, pl.ds(0, 3 * group)].reshape(3, group, rows, LANES)
            mc = main_r[m, kk, pl.ds(3 * group, 1)]
            q_below = north_r[m, kk, pl.ds(0, 3 * group)].reshape(3, group, 1, LANES)
            q_above = south_r[m, kk, pl.ds(0, 3 * group)].reshape(3, group, 1, LANES)
            mc_above = south_r[m, kk, pl.ds(3 * group, 1)][:, None, :]
            mc_n = jnp.where(sub == rows - 1, mc_above, pltpu.roll(mc, rows - 1, 1))
            parts = []
            for p in range(3):
                c_s, c_n = stow(mc, mc, width, p), stow(mc_n, mc_n, width, p)
                x = q[p]
                q_s = jnp.where(sub == 0, q_below[p], pltpu.roll(x, 1, 1))
                q_n = jnp.where(sub == rows - 1, q_above[p], pltpu.roll(x, rows - 1, 1))
                south = jnp.maximum(c_s, 0.0) * q_s + jnp.minimum(c_s, 0.0) * x
                north = jnp.maximum(c_n, 0.0) * x + jnp.minimum(c_n, 0.0) * q_n
                parts.append(x + south - north)
            parts.append(unstow(parts, width))
            for p in range(4):
                advected[m * levels + kk, pl.ds(p * group, group)] = parts[p]

    zc_copy.wait_recv()
    flow = jnp.zeros((bins, rows, LANES), jnp.float32)
    for k in range(n_lev * levels):
        t = thick_r[k // levels, pl.ds(k % levels, 1)]
        summed = advected[k] + flow
        settled = (t * inverse[k]) * summed
        flow = summed - settled
        z = jnp.where(lane == width, pltpu.roll(zc_r[:, k, :][None], width, 2), zc_s[:, k, :][None])
        west = jnp.maximum(z, 0.0) * pltpu.roll(settled, 1, 2) + jnp.minimum(z, 0.0) * settled
        moved = settled + west - pltpu.roll(west, LANES - 1, 2)
        coag = jnp.dot(kron[...], moved.reshape(cells, LANES), precision=HIGHEST,
                       preferred_element_type=jnp.float32).reshape(moved.shape)
        result = moved + dens[pl.ds(k, 1)] * moved * coag
        out_ref[:, :, k, :] = result[:, :, :width]

    below = jnp.zeros((rows, total), jnp.float32)
    for m in range(n_lev):
        @pl.when(j >= m)
        def _():
            tot_r[m] = jnp.zeros_like(tot_s)

        @pl.when(j < m)
        def _():
            pltpu.make_async_remote_copy(
                tot_s, tot_r.at[m], tot_ss.at[m], tot_rs.at[m], (i, m), MESH).wait_recv()

        below = below + tot_r[m][:, :total]
    for k in reversed(range(levels)):
        t = specific_air_factor * temp_ref[:, k, :] * span_ref[k]
        height_ref[:, k, :] = below + 0.5 * t
        below = below + t

    zc_copy.wait_send()
    for m in range(n_lev):
        @pl.when(j != m)
        def _():
            thick_copy(m).wait_send()
            main_copy(m).wait_send()

        @pl.when(j > m)
        def _():
            tot_copy(m).wait_send()

        @pl.when(has_south)
        def _():
            south_copy(m).wait_send()

        @pl.when(has_north)
        def _():
            north_copy(m).wait_send()


def hand_over(dust_ref, height_ref, dust_out, height_out, sem_out):
    pieces = sem_out.shape[0] - 1
    step = dust_ref.shape[0] // pieces
    leave = [pltpu.make_async_copy(height_ref, height_out, sem_out.at[pieces])]
    for p in range(pieces):
        part = pl.ds(p * step, step)
        leave.append(pltpu.make_async_copy(dust_ref.at[part], dust_out.at[part], sem_out.at[p]))
    for copy in leave:
        copy.start()
    for copy in leave:
        copy.wait()


def solution(mesh):
    n_lat, n_lev = mesh.shape["lat"], mesh.shape["lev"]
    vmem = pl.BlockSpec(memory_space=pltpu.VMEM)
    hbm = pl.BlockSpec(memory_space=pltpu.HBM)

    def on_device(q, mc, temp, span, fall, zc, rate):
        bins, rows, levels, total = q.shape
        width = total // n_lev
        assert width + 2 <= 3 * (LANES - 2 - width) and bins % 4 == 0
        packed = 3 * bins // 4 + 1
        deep = n_lev * levels
        wide = -(-total // LANES) * LANES
        f32 = jnp.float32
        main = pltpu.VMEM((n_lev, levels, packed, rows, LANES), f32)
        thick = pltpu.VMEM((n_lev, levels, rows, LANES), f32)
        edge = pltpu.VMEM((n_lev, levels, packed, LANES), f32)
        zonal = pltpu.VMEM((rows, deep, LANES), f32)
        sems = pltpu.SemaphoreType.DMA((n_lev,))
        pair = pltpu.SemaphoreType.DMA((2,))
        q, mc, temp, span, fall, zc, rate = (
            pltpu.with_memory_space_constraint(x, pltpu.HBM) for x in (q, mc, temp, span, fall, zc, rate))
        dust, height = pl.pallas_call(
            functools.partial(kernel, n_lat, n_lev),
            out_shape=(
                pltpu.VMEM((bins, rows, deep, width), f32),
                pltpu.VMEM((rows, levels, total), f32),
            ),
            in_specs=[hbm] * 7,
            out_specs=(vmem, vmem),
            scratch_shapes=[
                pltpu.VMEM(q.shape, f32), pltpu.VMEM(mc.shape, f32), pltpu.VMEM(temp.shape, f32),
                pltpu.SMEM(span.shape, f32), pltpu.SMEM(fall.shape, f32),
                pltpu.VMEM(zc.shape, f32), pltpu.VMEM(rate.shape, f32),
                main, main, thick, thick, edge, edge, edge, edge,
                pltpu.VMEM((rows, wide), f32), pltpu.VMEM((n_lev, rows, wide), f32),
                zonal, zonal,
                pltpu.VMEM((deep, bins, rows, LANES), f32),
                pltpu.VMEM((deep, bins, rows, LANES), f32),
                pltpu.VMEM((bins * rows, bins * rows), f32),
                pltpu.VMEM((deep, rows, LANES), f32),
            ] + [sems] * 10 + [pair] * 2 + [pltpu.SemaphoreType.DMA((7,))],
            compiler_params=pltpu.CompilerParams(
                collective_id=0, has_side_effects=True, vmem_limit_bytes=24 * 1024 * 1024),
        )(q, mc, temp, span, fall, zc, rate)
        return pl.pallas_call(
            hand_over,
            out_shape=(
                jax.ShapeDtypeStruct(dust.shape, f32), jax.ShapeDtypeStruct(height.shape, f32)),
            in_specs=[vmem, vmem],
            out_specs=(hbm, hbm),
            scratch_shapes=[pltpu.SemaphoreType.DMA((5,))],
            compiler_params=pltpu.CompilerParams(vmem_limit_bytes=24 * 1024 * 1024),
        )(dust, height)

    in_specs = (
        P(None, "lat", "lev", None),
        P("lat", "lev", None),
        P("lat", "lev", None),
        P("lev"),
        P(),
        P("lat", None, "lev"),
        P(),
    )
    out_specs = (P(None, "lat", None, "lev"), P("lat", "lev", None))
    return jax.shard_map(
        on_device, mesh=mesh, in_specs=in_specs, out_specs=out_specs, check_vma=False
    )
```

```python
import functools

import jax
import jax.numpy as jnp
from jax import lax
from jax.experimental import pallas as pl
from jax.experimental.pallas import tpu as pltpu
from jax.sharding import PartitionSpec as P

specific_air_factor = 0.0293
scale_height = 7.0
LANES = 128
TILE = 8
MESH = pl.DeviceIdType.MESH
HIGHEST = lax.Precision.HIGHEST


def widen(x):
    short = -x.shape[-1] % LANES
    if short:
        x = jnp.concatenate([x, jnp.zeros((*x.shape[:-1], short), x.dtype)], -1)
    return x


def lon_block(tile, total, width, block):
    count = -(-total // LANES)
    last = total % LANES
    start = block * width - 1
    c, off = start // LANES, start % LANES

    def piece(i):
        if i < 0:
            x = tile(count - 1)
            return pltpu.roll(x, (LANES - last) % LANES, x.ndim - 1)
        if i == count:
            return tile(0)
        x = tile(i)
        if i == count - 1 and last and total < start + width + 2:
            lane = lax.broadcasted_iota(jnp.int32, x.shape, x.ndim - 1)
            x = jnp.where(lane < last, x, pltpu.roll(tile(0), last, x.ndim - 1))
        return x

    x = piece(c)
    if off + width + 2 > LANES:
        lane = lax.broadcasted_iota(jnp.int32, x.shape, x.ndim - 1)
        x = jnp.where(lane >= off, x, piece(c + 1))
    return pltpu.roll(x, (2 * LANES - off - 1) % LANES, x.ndim - 1)


def row_pairs(rows):
    return [(r, r + 1) for r in range(1, rows - 1, 2)] + [(0, rows - 1)]


def kernel(
    n_lat, n_lev,
    q_hbm, mc_hbm, temp_hbm, span_hbm, fall_hbm, zc_hbm, rate_hbm,
    out_ref, height_ref,
    q_v, mc_v, temp_v, span_s, fall_s, zc_v, rate_v,
    main_s, main_r, thick_s, thick_r, south_r, north_r, mcn_r, below_s, below_r,
    halo_s, halo_r, adv_v, ratio_v, dens_v, z_v, merge_v,
    q_sem, load_sem, main_ss, main_rs, thick_ss, thick_rs,
    below_ss, below_rs, north_ss, north_rs, south_ss, south_rs, halo_sem,
):
    i, j = lax.axis_index("lat"), lax.axis_index("lev")
    rows, levels, bins, total = q_v.shape
    width = total // n_lev
    full = bins // TILE
    rest = bins % TILE
    body = full * TILE
    pairs = row_pairs(rows)
    stack = 2 * bins
    carriers = 2 * full
    deep = n_lev * levels
    piece = -(-(width + 2) // carriers)
    padded = -(-stack // 16) * 16
    count = -(-total // LANES)
    half_way = n_lev // 2
    has_south, has_north = i > 0, i < n_lat - 1
    left = lax.rem(j + n_lev - 1, n_lev)

    barrier = pltpu.get_barrier_semaphore()
    for d in range(1, n_lev):
        pl.semaphore_signal(barrier, inc=1, device_id=(i, lax.rem(j + d, n_lev)), device_id_type=MESH)

    @pl.when(has_south)
    def _():
        pl.semaphore_signal(barrier, inc=1, device_id=(i - 1, j), device_id_type=MESH)

    @pl.when(has_north)
    def _():
        pl.semaphore_signal(barrier, inc=1, device_id=(i + 1, j), device_id_type=MESH)

    small = [
        pltpu.make_async_copy(src, dst, load_sem.at[number])
        for number, (src, dst) in enumerate((
            (span_hbm, span_s), (temp_hbm, temp_v), (mc_hbm, mc_v), (zc_hbm, zc_v),
            (fall_hbm, fall_s), (rate_hbm, rate_v)))
    ]
    big = [[pltpu.make_async_copy(q_hbm.at[:, r, k, :], q_v.at[r, k], q_sem.at[r * levels + k])
            for k in range(levels)] for r in range(rows)]
    for load in small[:4]:
        load.start()
    order = list(dict.fromkeys(
        n for pair in pairs for r in pair for n in (r - 1, r, r + 1) if 0 <= n < rows))
    for r in order:
        for load in big[r]:
            load.start()
    for load in small[4:]:
        load.start()

    def main_copy(m, ch):
        return pltpu.make_async_remote_copy(
            main_s.at[m, ch], main_r.at[j, ch], main_ss.at[m, ch], main_rs.at[j, ch], (i, m), MESH)

    def main_arrival(m, ch):
        return pltpu.make_async_remote_copy(
            main_s.at[m, ch], main_r.at[m, ch], main_ss.at[m, ch], main_rs.at[m, ch], (i, m), MESH)

    def thick_copy(m):
        return pltpu.make_async_remote_copy(
            thick_s.at[m], thick_r.at[j], thick_ss.at[m], thick_rs.at[j], (i, m), MESH)

    def below_copy(m):
        return pltpu.make_async_remote_copy(
            below_s.at[m], below_r.at[j], below_ss.at[m], below_rs.at[j], (i, m), MESH)

    north_copies = [
        pltpu.make_async_remote_copy(
            q_hbm.at[:, rows - 1, k, :], south_r.at[k], north_ss.at[k], north_rs.at[k], (i + 1, j), MESH)
        for k in range(levels)]
    south_copies = [
        pltpu.make_async_remote_copy(
            q_hbm.at[:, 0, k, :], north_r.at[k], south_ss.at[k], south_rs.at[k], (i - 1, j), MESH)
        for k in range(levels)]
    south_copies.append(pltpu.make_async_remote_copy(
        mc_hbm.at[0], mcn_r, south_ss.at[levels], south_rs.at[levels], (i - 1, j), MESH))
    halo_copy = pltpu.make_async_remote_copy(
        halo_s, halo_r, halo_sem.at[0], halo_sem.at[1], (i, left), MESH)

    lane = lax.broadcasted_iota(jnp.int32, (TILE, LANES), 1)
    sub = lax.broadcasted_iota(jnp.int32, (TILE, LANES), 0)
    spare = (lane > width) & (lane <= width + piece)
    zlane = lax.broadcasted_iota(jnp.int32, (deep, LANES), 1)
    base = half_way * (j // half_way)
    far = [half_way - base + n for n in range(half_way)]
    near = [base + lax.rem(j - base + n, half_way) for n in range(1, half_way)]
    waited = set()

    def lanes_of(c):
        return slice(c * LANES, min((c + 1) * LANES, total))

    def prepare(ch):
        for r in order:
            if r not in waited and any(abs(r - r2) < 2 for r2 in pairs[ch]):
                waited.add(r)
                for load in big[r]:
                    load.wait()
        for k in range(levels):
            for c in range(count):
                at = lanes_of(c)
                for side, r in enumerate(pairs[ch]):
                    x = widen(q_v[r, k, :, at])
                    south = widen(q_v[r - 1, k, :, at] if r > 0 else south_r[k, :, at])
                    north = widen(q_v[r + 1, k, :, at] if r < rows - 1 else north_r[k, :, at])
                    c_s = widen(mc_v[r, k : k + 1, at])
                    c_n = widen(mc_v[r + 1, k : k + 1, at] if r < rows - 1 else mcn_r[k : k + 1, at])
                    keep = 1.0 + jnp.minimum(c_s, 0.0) - jnp.maximum(c_n, 0.0)
                    x = keep * x + jnp.maximum(c_s, 0.0) * south - jnp.minimum(c_n, 0.0) * north
                    adv_v[ch, k, c, side * body : (side + 1) * body] = x[:body]
                    low = 2 * body + side * rest
                    adv_v[ch, k, c, low : low + rest] = x[body:]
        for m in range(n_lev):
            for k in range(levels):
                x = lon_block(lambda c: adv_v[ch, k, c], total, width, m)
                extra = x[2 * body :]
                for p in range(carriers):
                    at = slice(p * TILE, (p + 1) * TILE)
                    main_s[m, ch, k, at] = jnp.where(
                        spare, pltpu.roll(extra, (width + 2 - piece * p) % LANES, 1), x[at])

    def send(ch):
        for m in far + near:
            main_copy(m, ch).start()
        main_r[pl.ds(j, 1), ch] = main_s[pl.ds(j, 1), ch]

    for load in small[:4]:
        load.wait()
    for k in range(levels):
        wide = widen(specific_air_factor * temp_v[:, k, :] * span_s[k])
        tile = lambda c: wide[:, c * LANES : (c + 1) * LANES]
        for m in range(n_lev):
            thick_s[m, k] = lon_block(tile, total, width, m)
    zc = widen(zc_v[...])
    halo = jnp.zeros((deep, LANES), jnp.float32)
    for r in range(rows):
        halo = jnp.where(zlane == r, pltpu.roll(zc[r], r, 1) if r else zc[r], halo)
        z_v[r] = zc[r]
    halo_s[...] = halo
    prepare(0)

    pl.semaphore_wait(barrier, n_lev - 1 + jnp.minimum(i, 1) + jnp.minimum(n_lat - 1 - i, 1))
    for m in far:
        thick_copy(m).start()
    for m in far:
        main_copy(m, 0).start()

    @pl.when(has_north)
    def _():
        for copy in north_copies:
            copy.start()

    @pl.when(has_south)
    def _():
        for copy in south_copies:
            copy.start()

    halo_copy.start()
    for m in near:
        thick_copy(m).start()
    for m in near:
        main_copy(m, 0).start()
    main_r[pl.ds(j, 1), 0] = main_s[pl.ds(j, 1), 0]
    thick_r[pl.ds(j, 1)] = thick_s[pl.ds(j, 1)]

    prepare(1)
    send(1)

    for load in small[4:]:
        load.wait()
    rate = rate_v[...]
    r0 = lax.broadcasted_iota(jnp.int32, rate.shape, 0)
    r1 = lax.broadcasted_iota(jnp.int32, rate.shape, 1)
    merging = jnp.where(r1 < r0, rate, jnp.where(r1 > r0, -rate, 0.0))

    def place(n):
        tail = n - 2 * body
        side = jnp.where(n < 2 * body, n // body, tail // rest)
        kind = jnp.where(n < 2 * body, n - side * body, body + tail - side * rest)
        return side, jnp.where(n < stack, kind, -1)

    _, kind = place(lax.broadcasted_iota(jnp.int32, (padded, bins), 0))
    pick = jnp.where(kind == lax.broadcasted_iota(jnp.int32, (padded, bins), 1), 1.0, 0.0)
    both = jnp.dot(pick, merging, precision=HIGHEST, preferred_element_type=jnp.float32)
    both = lax.dot_general(both, pick, (((1,), (1,)), ((), ())), precision=HIGHEST,
                           preferred_element_type=jnp.float32)
    side0, _ = place(lax.broadcasted_iota(jnp.int32, (padded, padded), 0))
    side1, _ = place(lax.broadcasted_iota(jnp.int32, (padded, padded), 1))
    both = jnp.where(side0 == side1, both, 0.0)
    high = both.astype(jnp.bfloat16)
    low = (both - high.astype(jnp.float32)).astype(jnp.bfloat16)
    merge_v[...] = jnp.concatenate([high, high, low], 1)

    def column(first, n):
        x = jnp.zeros((TILE, LANES), jnp.float32)
        for s in range(TILE):
            x = jnp.where(sub == s, fall_s[first + s % n], x)
        return x

    fall = [column(f * TILE, TILE) for f in range(full)]
    fall = jnp.concatenate(fall + fall + [column(body, rest)], 0)

    def spread(a, b):
        return jnp.concatenate([
            jnp.broadcast_to(a, (body, LANES)), jnp.broadcast_to(b, (body, LANES)),
            jnp.where(sub < rest, a, b)], 0)

    prepare(2)
    send(2)
    for ch in range(3, len(pairs) - 1):
        prepare(ch)
        send(ch)

    for m in range(n_lev):
        @pl.when(j != m)
        def _():
            pltpu.make_async_remote_copy(
                thick_s.at[m], thick_r.at[m], thick_ss.at[m], thick_rs.at[m], (i, m), MESH).wait_recv()
    below = jnp.zeros((rows, LANES), jnp.float32)
    for m in reversed(range(n_lev)):
        below_s[m] = below
        for k in reversed(range(levels)):
            t = thick_r[m, k]
            dens_v[m * levels + k] = jnp.exp((below + 0.5 * t) * (-1.0 / scale_height))
            below = below + t
    for m in far + near:
        below_copy(m).start()
    below_r[pl.ds(j, 1)] = below_s[pl.ds(j, 1)]

    for ch, (r, r2) in enumerate(pairs):
        for k in range(deep):
            t = spread(thick_r[k // levels, k % levels, r : r + 1], thick_r[k // levels, k % levels, r2 : r2 + 1])
            ratio_v[ch, k] = t / (t + fall)

    halo_copy.wait_recv()
    halo = halo_r[...]
    for r in range(rows):
        z_v[r] = jnp.where(zlane == width, pltpu.roll(halo, width - r, 1), z_v[r])

    def collect(ch):
        r, r2 = pairs[ch]
        flow = jnp.zeros((stack, LANES), jnp.float32)
        for group in range(0, n_lev, 2):
            for m in (group, group + 1):
                @pl.when(j != m)
                def _():
                    main_arrival(m, ch).wait_recv()

            moved = []
            ks = range(group * levels, (group + 2) * levels)
            for k in ks:
                x = main_r[k // levels, ch, k % levels]
                extra = None
                for p in reversed(range(carriers)):
                    part = pltpu.roll(x[p * TILE : (p + 1) * TILE], (piece * p - width - 2) % LANES, 1)
                    if extra is None:
                        extra = part
                    else:
                        first = lane < piece * (p + 1) - 1
                        extra = jnp.where(first | (lane == LANES - 1) if p == 0 else first, part, extra)
                x = jnp.concatenate([x, extra], 0)
                summed = x + flow
                settled = ratio_v[ch, k] * summed
                flow = summed - settled
                z, z2 = z_v[r, k : k + 1], z_v[r2, k : k + 1]
                up = spread(jnp.maximum(z, 0.0), jnp.maximum(z2, 0.0))
                down = spread(jnp.minimum(z, 0.0), jnp.minimum(z2, 0.0))
                west = up * pltpu.roll(settled, 1, 1) + down * settled
                moved.append(settled + west - pltpu.roll(west, LANES - 1, 1))
            x = jnp.concatenate(moved, 1)
            x = jnp.concatenate([x, jnp.zeros((padded - stack, x.shape[1]), jnp.float32)], 0)
            high = x.astype(jnp.bfloat16)
            low = (x - high.astype(jnp.float32)).astype(jnp.bfloat16)
            coag = jnp.dot(merge_v[...], jnp.concatenate([high, low, high], 0),
                           preferred_element_type=jnp.float32)
            for n, k in enumerate(ks):
                dens = spread(dens_v[k, r : r + 1], dens_v[k, r2 : r2 + 1])
                x = moved[n]
                x = (x + dens * x * coag[:stack, n * LANES : (n + 1) * LANES])[:, :width]
                out_ref[r, k, :body] = x[:body]
                out_ref[r2, k, :body] = x[body : 2 * body]
                out_ref[r, k, body:] = x[2 * body : 2 * body + rest]
                out_ref[r2, k, body:] = x[2 * body + rest :]

    @pl.when(jnp.logical_not(has_south))
    def _():
        south_r[...] = jnp.zeros_like(south_r)

    @pl.when(jnp.logical_not(has_north))
    def _():
        north_r[...] = jnp.zeros_like(north_r)
        mcn_r[...] = jnp.zeros_like(mcn_r)

    @pl.when(has_south)
    def _():
        for k in range(levels):
            pltpu.make_async_remote_copy(
                q_hbm.at[:, 0, k, :], south_r.at[k], north_ss.at[k], north_rs.at[k], (i - 1, j), MESH).wait_recv()

    @pl.when(has_north)
    def _():
        for k in range(levels):
            pltpu.make_async_remote_copy(
                q_hbm.at[:, 0, k, :], north_r.at[k], south_ss.at[k], south_rs.at[k], (i + 1, j), MESH).wait_recv()
        pltpu.make_async_remote_copy(
            mc_hbm.at[0], mcn_r, south_ss.at[levels], south_rs.at[levels], (i + 1, j), MESH).wait_recv()

    final = len(pairs) - 1
    prepare(final)
    send(final)
    for ch in range(final):
        collect(ch)

    for m in range(n_lev):
        @pl.when(j != m)
        def _():
            pltpu.make_async_remote_copy(
                below_s.at[m], below_r.at[m], below_ss.at[m], below_rs.at[m], (i, m), MESH).wait_recv()
    lower = []
    for c in range(count):
        x = jnp.zeros((rows, LANES), jnp.float32)
        for m in range(n_lev):
            first, end = m * width - c * LANES, (m + 1) * width - c * LANES
            if first < LANES and end > 0:
                x = jnp.where((lane >= first) & (lane < end), pltpu.roll(below_r[m], first % LANES, 1), x)
        lower.append(x)
    below = jnp.concatenate(lower, 1)[:, :total]
    for k in reversed(range(levels)):
        t = specific_air_factor * temp_v[:, k, :] * span_s[k]
        height_ref[:, k, :] = below + 0.5 * t
        below = below + t

    halo_copy.wait_send()
    for m in far + near:
        thick_copy(m).wait_send()
        below_copy(m).wait_send()
        for ch in range(final):
            main_copy(m, ch).wait_send()

    @pl.when(has_south)
    def _():
        for copy in south_copies:
            copy.wait_send()

    @pl.when(has_north)
    def _():
        for copy in north_copies:
            copy.wait_send()

    collect(final)
    for m in far + near:
        main_copy(m, final).wait_send()


def hand_over(dust_ref, height_ref, dust_out, height_out, sem_out):
    rows, deep = dust_ref.shape[:2]
    leave = [pltpu.make_async_copy(height_ref, height_out, sem_out.at[rows * deep])]
    for r in range(rows):
        for k in range(deep):
            leave.append(pltpu.make_async_copy(
                dust_ref.at[r, k], dust_out.at[:, r, k, :], sem_out.at[r * deep + k]))
    for copy in leave:
        copy.start()
    for copy in leave:
        copy.wait()


def solution(mesh):
    n_lat, n_lev = mesh.shape["lat"], mesh.shape["lev"]
    vmem = pl.BlockSpec(memory_space=pltpu.VMEM)
    hbm = pl.BlockSpec(memory_space=pltpu.HBM)

    def on_device(*args):
        bins, rows, levels, total = args[0].shape
        width = total // n_lev
        full, rest = bins // 8, bins % 8
        carriers = 2 * full
        piece = -(-(width + 2) // carriers)
        assert rest == 4 and rows == 8 and width + 1 + piece < LANES and n_lev % 2 == 0
        deep = n_lev * levels
        count = -(-total // LANES)
        chunks = len(row_pairs(rows))
        stack = 2 * bins
        padded = -(-stack // 16) * 16
        f32 = jnp.float32
        main = pltpu.VMEM((n_lev, chunks, levels, carriers * TILE, LANES), f32)
        thick = pltpu.VMEM((n_lev, levels, rows, LANES), f32)
        edge = pltpu.VMEM((levels, bins, total), f32)
        tile = pltpu.VMEM((n_lev, rows, LANES), f32)
        halo = pltpu.VMEM((deep, LANES), f32)
        dma = pltpu.SemaphoreType.DMA
        args = [pltpu.with_memory_space_constraint(x, pltpu.HBM) for x in args]
        dust, height = pl.pallas_call(
            functools.partial(kernel, n_lat, n_lev),
            out_shape=(
                pltpu.VMEM((rows, deep, bins, width), f32),
                pltpu.VMEM((rows, levels, total), f32),
            ),
            in_specs=[hbm] * 7,
            out_specs=(vmem, vmem),
            scratch_shapes=[
                pltpu.VMEM((rows, levels, bins, total), f32),
                pltpu.VMEM((rows, levels, total), f32), pltpu.VMEM((rows, levels, total), f32),
                pltpu.SMEM((levels,), f32), pltpu.SMEM((bins,), f32),
                pltpu.VMEM((rows, deep, width), f32), pltpu.VMEM((bins, bins), f32),
                main, main, thick, thick, edge, edge, pltpu.VMEM((levels, total), f32), tile, tile,
                halo, halo,
                pltpu.VMEM((chunks, levels, count, stack, LANES), f32),
                pltpu.VMEM((chunks, deep, stack, LANES), f32),
                pltpu.VMEM((deep, rows, LANES), f32),
                pltpu.VMEM((rows, deep, LANES), f32),
                                pltpu.VMEM((padded, 3 * padded), jnp.bfloat16),
                dma((rows * levels,)), dma((6,)),
                dma((n_lev, chunks)), dma((n_lev, chunks)),
                dma((n_lev,)), dma((n_lev,)), dma((n_lev,)), dma((n_lev,)),
                dma((levels,)), dma((levels,)), dma((levels + 1,)), dma((levels + 1,)), dma((2,)),
            ],
            compiler_params=pltpu.CompilerParams(
                collective_id=0, has_side_effects=True, vmem_limit_bytes=32 * 1024 * 1024),
        )(*args)
        return pl.pallas_call(
            hand_over,
            out_shape=(
                jax.ShapeDtypeStruct((bins, rows, deep, width), f32),
                jax.ShapeDtypeStruct(height.shape, f32)),
            in_specs=[vmem, vmem],
            out_specs=(hbm, hbm),
            scratch_shapes=[dma((rows * deep + 1,))],
            compiler_params=pltpu.CompilerParams(vmem_limit_bytes=32 * 1024 * 1024),
        )(dust, height)

    in_specs = (
        P(None, "lat", "lev", None),
        P("lat", "lev", None),
        P("lat", "lev", None),
        P("lev"),
        P(),
        P("lat", None, "lev"),
        P(),
    )
    out_specs = (P(None, "lat", None, "lev"), P("lat", "lev", None))
    return jax.shard_map(
        on_device, mesh=mesh, in_specs=in_specs, out_specs=out_specs, check_vma=False
    )
```

```python
import functools

import jax
import jax.numpy as jnp
from jax import lax
from jax.experimental import pallas as pl
from jax.experimental.pallas import tpu as pltpu
from jax.sharding import PartitionSpec as P

specific_air_factor = 0.0293
scale_height = 7.0
LANES = 128
TILE = 8
MESH = pl.DeviceIdType.MESH
HIGHEST = lax.Precision.HIGHEST


def widen(x):
    short = -x.shape[-1] % LANES
    if short:
        x = jnp.concatenate([x, jnp.zeros((*x.shape[:-1], short), x.dtype)], -1)
    return x


def lon_block(tile, total, width, block):
    count = -(-total // LANES)
    last = total % LANES
    start = block * width - 1
    c, off = start // LANES, start % LANES

    def piece(i):
        if i < 0:
            x = tile(count - 1)
            return pltpu.roll(x, (LANES - last) % LANES, x.ndim - 1)
        if i == count:
            return tile(0)
        x = tile(i)
        if i == count - 1 and last and total < start + width + 2:
            lane = lax.broadcasted_iota(jnp.int32, x.shape, x.ndim - 1)
            x = jnp.where(lane < last, x, pltpu.roll(tile(0), last, x.ndim - 1))
        return x

    x = piece(c)
    if off + width + 2 > LANES:
        lane = lax.broadcasted_iota(jnp.int32, x.shape, x.ndim - 1)
        x = jnp.where(lane >= off, x, piece(c + 1))
    return pltpu.roll(x, (2 * LANES - off - 1) % LANES, x.ndim - 1)


def row_pairs(rows):
    return [(r, r + 1) for r in range(1, rows - 1, 2)] + [(0, rows - 1)]


def kernel(
    n_lat, n_lev,
    q_hbm, mc_hbm, temp_hbm, span_hbm, fall_hbm, zc_hbm, rate_hbm,
    out_ref, height_ref,
    q_v, mc_v, temp_v, span_s, fall_s, zc_v, rate_v,
    main_s, main_r, thick_s, thick_r, south_r, north_r, mcn_r, below_s, below_r,
    halo_s, halo_r, adv_v, ratio_v, dens_v, z_v, merge_v,
    q_sem, load_sem, main_ss, main_rs, thick_ss, thick_rs,
    below_ss, below_rs, north_ss, north_rs, south_ss, south_rs, halo_sem,
):
    i, j = lax.axis_index("lat"), lax.axis_index("lev")
    rows, levels, bins, total = q_v.shape
    width = total // n_lev
    full = bins // TILE
    rest = bins % TILE
    body = full * TILE
    pairs = row_pairs(rows)
    stack = 2 * bins
    carriers = 2 * full
    deep = n_lev * levels
    piece = -(-(width + 2) // carriers)
    padded = -(-stack // 16) * 16
    count = -(-total // LANES)
    half_way = n_lev // 2
    has_south, has_north = i > 0, i < n_lat - 1
    left = lax.rem(j + n_lev - 1, n_lev)

    barrier = pltpu.get_barrier_semaphore()
    for d in range(1, n_lev):
        pl.semaphore_signal(barrier, inc=1, device_id=(i, lax.rem(j + d, n_lev)), device_id_type=MESH)

    @pl.when(has_south)
    def _():
        pl.semaphore_signal(barrier, inc=1, device_id=(i - 1, j), device_id_type=MESH)

    @pl.when(has_north)
    def _():
        pl.semaphore_signal(barrier, inc=1, device_id=(i + 1, j), device_id_type=MESH)

    small = [
        pltpu.make_async_copy(src, dst, load_sem.at[number])
        for number, (src, dst) in enumerate((
            (span_hbm, span_s), (temp_hbm, temp_v), (mc_hbm, mc_v), (zc_hbm, zc_v),
            (fall_hbm, fall_s), (rate_hbm, rate_v)))
    ]
    big = [[pltpu.make_async_copy(q_hbm.at[:, r, k, :], q_v.at[r, k], q_sem.at[r * levels + k])
            for k in range(levels)] for r in range(rows)]
    for load in small[:4]:
        load.start()
    order = list(dict.fromkeys(
        n for pair in pairs for r in pair for n in (r - 1, r, r + 1) if 0 <= n < rows))
    for r in order:
        for load in big[r]:
            load.start()
    for load in small[4:]:
        load.start()

    def main_copy(m, ch):
        return pltpu.make_async_remote_copy(
            main_s.at[m, ch], main_r.at[j, ch], main_ss.at[m, ch], main_rs.at[j, ch], (i, m), MESH)

    def main_arrival(m, ch):
        return pltpu.make_async_remote_copy(
            main_s.at[m, ch], main_r.at[m, ch], main_ss.at[m, ch], main_rs.at[m, ch], (i, m), MESH)

    def thick_copy(m):
        return pltpu.make_async_remote_copy(
            thick_s.at[m], thick_r.at[j], thick_ss.at[m], thick_rs.at[j], (i, m), MESH)

    def below_copy(m):
        return pltpu.make_async_remote_copy(
            below_s.at[m], below_r.at[j], below_ss.at[m], below_rs.at[j], (i, m), MESH)

    north_copies = [
        pltpu.make_async_remote_copy(
            q_hbm.at[:, rows - 1, k, :], south_r.at[k], north_ss.at[k], north_rs.at[k], (i + 1, j), MESH)
        for k in range(levels)]
    south_copies = [
        pltpu.make_async_remote_copy(
            q_hbm.at[:, 0, k, :], north_r.at[k], south_ss.at[k], south_rs.at[k], (i - 1, j), MESH)
        for k in range(levels)]
    south_copies.append(pltpu.make_async_remote_copy(
        mc_hbm.at[0], mcn_r, south_ss.at[levels], south_rs.at[levels], (i - 1, j), MESH))
    halo_copy = pltpu.make_async_remote_copy(
        halo_s, halo_r, halo_sem.at[0], halo_sem.at[1], (i, left), MESH)

    lane = lax.broadcasted_iota(jnp.int32, (TILE, LANES), 1)
    sub = lax.broadcasted_iota(jnp.int32, (TILE, LANES), 0)
    spare = (lane > width) & (lane <= width + piece)
    zlane = lax.broadcasted_iota(jnp.int32, (deep, LANES), 1)
    base = half_way * (j // half_way)
    far = [half_way - base + n for n in range(half_way)]
    near = [base + lax.rem(j - base + n, half_way) for n in range(1, half_way)]
    waited = set()

    def lanes_of(c):
        return slice(c * LANES, min((c + 1) * LANES, total))

    def prepare(ch):
        for r in order:
            if r not in waited and any(abs(r - r2) < 2 for r2 in pairs[ch]):
                waited.add(r)
                for load in big[r]:
                    load.wait()
        for k in range(levels):
            for c in range(count):
                at = lanes_of(c)
                for side, r in enumerate(pairs[ch]):
                    x = widen(q_v[r, k, :, at])
                    south = widen(q_v[r - 1, k, :, at] if r > 0 else south_r[k, :, at])
                    north = widen(q_v[r + 1, k, :, at] if r < rows - 1 else north_r[k, :, at])
                    c_s = widen(mc_v[r, k : k + 1, at])
                    c_n = widen(mc_v[r + 1, k : k + 1, at] if r < rows - 1 else mcn_r[k : k + 1, at])
                    keep = 1.0 + jnp.minimum(c_s, 0.0) - jnp.maximum(c_n, 0.0)
                    x = keep * x + jnp.maximum(c_s, 0.0) * south - jnp.minimum(c_n, 0.0) * north
                    adv_v[ch, k, c, side * body : (side + 1) * body] = x[:body]
                    low = 2 * body + side * rest
                    adv_v[ch, k, c, low : low + rest] = x[body:]
        for m in range(n_lev):
            for k in range(levels):
                x = lon_block(lambda c: adv_v[ch, k, c], total, width, m)
                extra = x[2 * body :]
                for p in range(carriers):
                    at = slice(p * TILE, (p + 1) * TILE)
                    main_s[m, ch, k, at] = jnp.where(
                        spare, pltpu.roll(extra, (width + 2 - piece * p) % LANES, 1), x[at])

    def send(ch):
        for m in far + near:
            main_copy(m, ch).start()
        main_r[pl.ds(j, 1), ch] = main_s[pl.ds(j, 1), ch]

    for load in small[:4]:
        load.wait()
    for k in range(levels):
        wide = widen(specific_air_factor * temp_v[:, k, :] * span_s[k])
        tile = lambda c: wide[:, c * LANES : (c + 1) * LANES]
        for m in range(n_lev):
            thick_s[m, k] = lon_block(tile, total, width, m)
    zc = widen(zc_v[...])
    halo = jnp.zeros((deep, LANES), jnp.float32)
    for r in range(rows):
        halo = jnp.where(zlane == r, pltpu.roll(zc[r], r, 1) if r else zc[r], halo)
        z_v[r] = zc[r]
    halo_s[...] = halo
    prepare(0)

    pl.semaphore_wait(barrier, n_lev - 1 + jnp.minimum(i, 1) + jnp.minimum(n_lat - 1 - i, 1))
    for m in far:
        thick_copy(m).start()
    for m in far:
        main_copy(m, 0).start()

    @pl.when(has_north)
    def _():
        for copy in north_copies:
            copy.start()

    @pl.when(has_south)
    def _():
        for copy in south_copies:
            copy.start()

    halo_copy.start()
    for m in near:
        thick_copy(m).start()
    for m in near:
        main_copy(m, 0).start()
    main_r[pl.ds(j, 1), 0] = main_s[pl.ds(j, 1), 0]
    thick_r[pl.ds(j, 1)] = thick_s[pl.ds(j, 1)]

    prepare(1)
    send(1)

    for load in small[4:]:
        load.wait()
    rate = rate_v[...]
    r0 = lax.broadcasted_iota(jnp.int32, rate.shape, 0)
    r1 = lax.broadcasted_iota(jnp.int32, rate.shape, 1)
    merging = jnp.where(r1 < r0, rate, jnp.where(r1 > r0, -rate, 0.0))

    def place(n):
        tail = n - 2 * body
        side = jnp.where(n < 2 * body, n // body, tail // rest)
        kind = jnp.where(n < 2 * body, n - side * body, body + tail - side * rest)
        return side, jnp.where(n < stack, kind, -1)

    _, kind = place(lax.broadcasted_iota(jnp.int32, (padded, bins), 0))
    pick = jnp.where(kind == lax.broadcasted_iota(jnp.int32, (padded, bins), 1), 1.0, 0.0)
    both = jnp.dot(pick, merging, precision=HIGHEST, preferred_element_type=jnp.float32)
    both = lax.dot_general(both, pick, (((1,), (1,)), ((), ())), precision=HIGHEST,
                           preferred_element_type=jnp.float32)
    side0, _ = place(lax.broadcasted_iota(jnp.int32, (padded, padded), 0))
    side1, _ = place(lax.broadcasted_iota(jnp.int32, (padded, padded), 1))
    both = jnp.where(side0 == side1, both, 0.0)
    high = both.astype(jnp.bfloat16)
    low = (both - high.astype(jnp.float32)).astype(jnp.bfloat16)
    merge_v[...] = jnp.concatenate([high, high, low], 1)

    def column(first, n):
        x = jnp.zeros((TILE, LANES), jnp.float32)
        for s in range(TILE):
            x = jnp.where(sub == s, fall_s[first + s % n], x)
        return x

    fall = [column(f * TILE, TILE) for f in range(full)]
    fall = jnp.concatenate(fall + fall + [column(body, rest)], 0)

    def spread(a, b):
        return jnp.concatenate([
            jnp.broadcast_to(a, (body, LANES)), jnp.broadcast_to(b, (body, LANES)),
            jnp.where(sub < rest, a, b)], 0)

    prepare(2)
    send(2)
    for ch in range(3, len(pairs) - 1):
        prepare(ch)
        send(ch)

    for m in range(n_lev):
        @pl.when(j != m)
        def _():
            pltpu.make_async_remote_copy(
                thick_s.at[m], thick_r.at[m], thick_ss.at[m], thick_rs.at[m], (i, m), MESH).wait_recv()
    below = jnp.zeros((rows, LANES), jnp.float32)
    for m in reversed(range(n_lev)):
        below_s[m] = below
        for k in reversed(range(levels)):
            t = thick_r[m, k]
            dens_v[m * levels + k] = jnp.exp((below + 0.5 * t) * (-1.0 / scale_height))
            below = below + t
    for m in far + near:
        below_copy(m).start()
    below_r[pl.ds(j, 1)] = below_s[pl.ds(j, 1)]

    for ch, (r, r2) in enumerate(pairs):
        for k in range(deep):
            t = spread(thick_r[k // levels, k % levels, r : r + 1], thick_r[k // levels, k % levels, r2 : r2 + 1])
            ratio_v[ch, k] = t / (t + fall)

    halo_copy.wait_recv()
    halo = halo_r[...]
    for r in range(rows):
        z_v[r] = jnp.where(zlane == width, pltpu.roll(halo, width - r, 1), z_v[r])

    def collect(ch):
        r, r2 = pairs[ch]
        flow = jnp.zeros((stack, LANES), jnp.float32)
        for group in range(0, n_lev, 2):
            for m in (group, group + 1):
                @pl.when(j != m)
                def _():
                    main_arrival(m, ch).wait_recv()

            moved = []
            ks = range(group * levels, (group + 2) * levels)
            for k in ks:
                x = main_r[k // levels, ch, k % levels]
                extra = None
                for p in reversed(range(carriers)):
                    part = pltpu.roll(x[p * TILE : (p + 1) * TILE], (piece * p - width - 2) % LANES, 1)
                    if extra is None:
                        extra = part
                    else:
                        first = lane < piece * (p + 1) - 1
                        extra = jnp.where(first | (lane == LANES - 1) if p == 0 else first, part, extra)
                x = jnp.concatenate([x, extra], 0)
                summed = x + flow
                settled = ratio_v[ch, k] * summed
                flow = summed - settled
                z, z2 = z_v[r, k : k + 1], z_v[r2, k : k + 1]
                up = spread(jnp.maximum(z, 0.0), jnp.maximum(z2, 0.0))
                down = spread(jnp.minimum(z, 0.0), jnp.minimum(z2, 0.0))
                west = up * pltpu.roll(settled, 1, 1) + down * settled
                moved.append(settled + west - pltpu.roll(west, LANES - 1, 1))
            x = jnp.concatenate(moved, 1)
            x = jnp.concatenate([x, jnp.zeros((padded - stack, x.shape[1]), jnp.float32)], 0)
            high = x.astype(jnp.bfloat16)
            low = (x - high.astype(jnp.float32)).astype(jnp.bfloat16)
            coag = jnp.dot(merge_v[...], jnp.concatenate([high, low, high], 0),
                           preferred_element_type=jnp.float32)
            for n, k in enumerate(ks):
                dens = spread(dens_v[k, r : r + 1], dens_v[k, r2 : r2 + 1])
                x = moved[n]
                x = (x + dens * x * coag[:stack, n * LANES : (n + 1) * LANES])[:, :width]
                out_ref[:body, r, k, :] = x[:body]
                out_ref[:body, r2, k, :] = x[body : 2 * body]
                out_ref[body:, r, k, :] = x[2 * body : 2 * body + rest]
                out_ref[body:, r2, k, :] = x[2 * body + rest :]

    @pl.when(jnp.logical_not(has_south))
    def _():
        south_r[...] = jnp.zeros_like(south_r)

    @pl.when(jnp.logical_not(has_north))
    def _():
        north_r[...] = jnp.zeros_like(north_r)
        mcn_r[...] = jnp.zeros_like(mcn_r)

    @pl.when(has_south)
    def _():
        for k in range(levels):
            pltpu.make_async_remote_copy(
                q_hbm.at[:, 0, k, :], south_r.at[k], north_ss.at[k], north_rs.at[k], (i - 1, j), MESH).wait_recv()

    @pl.when(has_north)
    def _():
        for k in range(levels):
            pltpu.make_async_remote_copy(
                q_hbm.at[:, 0, k, :], north_r.at[k], south_ss.at[k], south_rs.at[k], (i + 1, j), MESH).wait_recv()
        pltpu.make_async_remote_copy(
            mc_hbm.at[0], mcn_r, south_ss.at[levels], south_rs.at[levels], (i + 1, j), MESH).wait_recv()

    final = len(pairs) - 1
    prepare(final)
    send(final)
    for ch in range(final):
        collect(ch)

    for m in range(n_lev):
        @pl.when(j != m)
        def _():
            pltpu.make_async_remote_copy(
                below_s.at[m], below_r.at[m], below_ss.at[m], below_rs.at[m], (i, m), MESH).wait_recv()
    lower = []
    for c in range(count):
        x = jnp.zeros((rows, LANES), jnp.float32)
        for m in range(n_lev):
            first, end = m * width - c * LANES, (m + 1) * width - c * LANES
            if first < LANES and end > 0:
                x = jnp.where((lane >= first) & (lane < end), pltpu.roll(below_r[m], first % LANES, 1), x)
        lower.append(x)
    below = jnp.concatenate(lower, 1)[:, :total]
    for k in reversed(range(levels)):
        t = specific_air_factor * temp_v[:, k, :] * span_s[k]
        height_ref[:, k, :] = below + 0.5 * t
        below = below + t

    halo_copy.wait_send()
    for m in far + near:
        thick_copy(m).wait_send()
        below_copy(m).wait_send()
        for ch in range(final):
            main_copy(m, ch).wait_send()

    @pl.when(has_south)
    def _():
        for copy in south_copies:
            copy.wait_send()

    @pl.when(has_north)
    def _():
        for copy in north_copies:
            copy.wait_send()

    collect(final)
    for m in far + near:
        main_copy(m, final).wait_send()


def hand_over(dust_ref, height_ref, dust_out, height_out, sem_out):
    pieces = sem_out.shape[0] - 1
    step = dust_ref.shape[0] // pieces
    leave = []
    for p in range(pieces):
        part = pl.ds(p * step, step)
        leave.append(pltpu.make_async_copy(dust_ref.at[part], dust_out.at[part], sem_out.at[p]))
    leave.append(pltpu.make_async_copy(height_ref, height_out, sem_out.at[pieces]))
    for copy in leave:
        copy.start()
    for copy in leave:
        copy.wait()


def solution(mesh):
    n_lat, n_lev = mesh.shape["lat"], mesh.shape["lev"]
    vmem = pl.BlockSpec(memory_space=pltpu.VMEM)
    hbm = pl.BlockSpec(memory_space=pltpu.HBM)

    def on_device(*args):
        bins, rows, levels, total = args[0].shape
        width = total // n_lev
        full, rest = bins // 8, bins % 8
        carriers = 2 * full
        piece = -(-(width + 2) // carriers)
        assert rest == 4 and rows == 8 and width + 1 + piece < LANES and n_lev % 2 == 0
        deep = n_lev * levels
        count = -(-total // LANES)
        chunks = len(row_pairs(rows))
        stack = 2 * bins
        padded = -(-stack // 16) * 16
        f32 = jnp.float32
        main = pltpu.VMEM((n_lev, chunks, levels, carriers * TILE, LANES), f32)
        thick = pltpu.VMEM((n_lev, levels, rows, LANES), f32)
        edge = pltpu.VMEM((levels, bins, total), f32)
        tile = pltpu.VMEM((n_lev, rows, LANES), f32)
        halo = pltpu.VMEM((deep, LANES), f32)
        dma = pltpu.SemaphoreType.DMA
        args = [pltpu.with_memory_space_constraint(x, pltpu.HBM) for x in args]
        dust, height = pl.pallas_call(
            functools.partial(kernel, n_lat, n_lev),
            out_shape=(
                pltpu.VMEM((bins, rows, deep, width), f32),
                pltpu.VMEM((rows, levels, total), f32),
            ),
            in_specs=[hbm] * 7,
            out_specs=(vmem, vmem),
            scratch_shapes=[
                pltpu.VMEM((rows, levels, bins, total), f32),
                pltpu.VMEM((rows, levels, total), f32), pltpu.VMEM((rows, levels, total), f32),
                pltpu.SMEM((levels,), f32), pltpu.SMEM((bins,), f32),
                pltpu.VMEM((rows, deep, width), f32), pltpu.VMEM((bins, bins), f32),
                main, main, thick, thick, edge, edge, pltpu.VMEM((levels, total), f32), tile, tile,
                halo, halo,
                pltpu.VMEM((chunks, levels, count, stack, LANES), f32),
                pltpu.VMEM((chunks, deep, stack, LANES), f32),
                pltpu.VMEM((deep, rows, LANES), f32),
                pltpu.VMEM((rows, deep, LANES), f32),
                                pltpu.VMEM((padded, 3 * padded), jnp.bfloat16),
                dma((rows * levels,)), dma((6,)),
                dma((n_lev, chunks)), dma((n_lev, chunks)),
                dma((n_lev,)), dma((n_lev,)), dma((n_lev,)), dma((n_lev,)),
                dma((levels,)), dma((levels,)), dma((levels + 1,)), dma((levels + 1,)), dma((2,)),
            ],
            compiler_params=pltpu.CompilerParams(
                collective_id=0, has_side_effects=True, vmem_limit_bytes=32 * 1024 * 1024),
        )(*args)
        return pl.pallas_call(
            hand_over,
            out_shape=(
                jax.ShapeDtypeStruct((bins, rows, deep, width), f32),
                jax.ShapeDtypeStruct(height.shape, f32)),
            in_specs=[vmem, vmem],
            out_specs=(hbm, hbm),
            scratch_shapes=[dma((5,))],
            compiler_params=pltpu.CompilerParams(vmem_limit_bytes=32 * 1024 * 1024),
        )(dust, height)

    in_specs = (
        P(None, "lat", "lev", None),
        P("lat", "lev", None),
        P("lat", "lev", None),
        P("lev"),
        P(),
        P("lat", None, "lev"),
        P(),
    )
    out_specs = (P(None, "lat", None, "lev"), P("lat", "lev", None))
    return jax.shard_map(
        on_device, mesh=mesh, in_specs=in_specs, out_specs=out_specs, check_vma=False
    )
```

```python
import functools

import jax
import jax.numpy as jnp
from jax import lax
from jax.experimental import pallas as pl
from jax.experimental.pallas import tpu as pltpu
from jax.sharding import PartitionSpec as P

specific_air_factor = 0.0293
scale_height = 7.0
LANES = 128
TILE = 8
MESH = pl.DeviceIdType.MESH
HIGHEST = lax.Precision.HIGHEST


def widen(x):
    short = -x.shape[-1] % LANES
    if short:
        x = jnp.concatenate([x, jnp.zeros((*x.shape[:-1], short), x.dtype)], -1)
    return x


def lon_block(tile, total, width, block):
    count = -(-total // LANES)
    last = total % LANES
    start = block * width - 1
    c, off = start // LANES, start % LANES

    def piece(i):
        if i < 0:
            x = tile(count - 1)
            return pltpu.roll(x, (LANES - last) % LANES, x.ndim - 1)
        if i == count:
            return tile(0)
        x = tile(i)
        if i == count - 1 and last and total < start + width + 2:
            lane = lax.broadcasted_iota(jnp.int32, x.shape, x.ndim - 1)
            x = jnp.where(lane < last, x, pltpu.roll(tile(0), last, x.ndim - 1))
        return x

    x = piece(c)
    if off + width + 2 > LANES:
        lane = lax.broadcasted_iota(jnp.int32, x.shape, x.ndim - 1)
        x = jnp.where(lane >= off, x, piece(c + 1))
    return pltpu.roll(x, (2 * LANES - off - 1) % LANES, x.ndim - 1)


def row_pairs(rows):
    return [(r, r + 1) for r in range(1, rows - 1, 2)] + [(0, rows - 1)]


def kernel(
    n_lat, n_lev,
    q_hbm, mc_hbm, temp_hbm, span_hbm, fall_hbm, zc_hbm, rate_hbm,
    out_ref, height_ref,
    q_v, mc_v, temp_v, span_s, fall_s, zc_v, rate_v,
    main_s, main_r, thick_s, thick_r, south_r, north_r, mcn_r, below_s, below_r,
    halo_s, halo_r, adv_v, ratio_v, dens_v, full_v, z_v, merge_v,
    q_sem, load_sem, main_ss, main_rs, thick_ss, thick_rs,
    below_ss, below_rs, north_ss, north_rs, south_ss, south_rs, halo_sem,
):
    i, j = lax.axis_index("lat"), lax.axis_index("lev")
    rows, levels, bins, total = q_v.shape
    width = total // n_lev
    full = bins // TILE
    rest = bins % TILE
    body = full * TILE
    pairs = row_pairs(rows)
    stack = 2 * bins
    deep = n_lev * levels
    piece = -(-(width + 2) // 3)
    base_row, ends = 6 * TILE, slice(7 * TILE, 7 * TILE + TILE // 2)
    padded = -(-stack // 16) * 16
    count = -(-total // LANES)
    half_way = n_lev // 2
    has_south, has_north = i > 0, i < n_lat - 1
    left = lax.rem(j + n_lev - 1, n_lev)

    barrier = pltpu.get_barrier_semaphore()
    for d in range(1, n_lev):
        pl.semaphore_signal(barrier, inc=1, device_id=(i, lax.rem(j + d, n_lev)), device_id_type=MESH)

    @pl.when(has_south)
    def _():
        pl.semaphore_signal(barrier, inc=1, device_id=(i - 1, j), device_id_type=MESH)

    @pl.when(has_north)
    def _():
        pl.semaphore_signal(barrier, inc=1, device_id=(i + 1, j), device_id_type=MESH)

    small = [
        pltpu.make_async_copy(src, dst, load_sem.at[number])
        for number, (src, dst) in enumerate((
            (span_hbm, span_s), (temp_hbm, temp_v), (mc_hbm, mc_v), (zc_hbm, zc_v),
            (fall_hbm, fall_s), (rate_hbm, rate_v)))
    ]
    big = [[pltpu.make_async_copy(q_hbm.at[:, r, k, :], q_v.at[r, k], q_sem.at[r * levels + k])
            for k in range(levels)] for r in range(rows)]
    for load in small[:4]:
        load.start()
    order = list(dict.fromkeys(
        n for pair in pairs for r in pair for n in (r - 1, r, r + 1) if 0 <= n < rows))
    for r in order:
        for load in big[r]:
            load.start()
    for load in small[4:]:
        load.start()

    def main_copy(m, ch):
        return pltpu.make_async_remote_copy(
            main_s.at[m, ch], main_r.at[j, ch], main_ss.at[m, ch], main_rs.at[j, ch], (i, m), MESH)

    def main_arrival(m, ch):
        return pltpu.make_async_remote_copy(
            main_s.at[m, ch], main_r.at[m, ch], main_ss.at[m, ch], main_rs.at[m, ch], (i, m), MESH)

    def thick_copy(m):
        return pltpu.make_async_remote_copy(
            thick_s.at[m], thick_r.at[j], thick_ss.at[m], thick_rs.at[j], (i, m), MESH)

    def below_copy(m):
        return pltpu.make_async_remote_copy(
            below_s.at[m], below_r.at[j], below_ss.at[m], below_rs.at[j], (i, m), MESH)

    north_copies = [
        pltpu.make_async_remote_copy(
            q_hbm.at[:, rows - 1, k, :], south_r.at[k], north_ss.at[k], north_rs.at[k], (i + 1, j), MESH)
        for k in range(levels)]
    south_copies = [
        pltpu.make_async_remote_copy(
            q_hbm.at[:, 0, k, :], north_r.at[k], south_ss.at[k], south_rs.at[k], (i - 1, j), MESH)
        for k in range(levels)]
    south_copies.append(pltpu.make_async_remote_copy(
        mc_hbm.at[0], mcn_r, south_ss.at[levels], south_rs.at[levels], (i - 1, j), MESH))
    halo_copy = pltpu.make_async_remote_copy(
        halo_s, halo_r, halo_sem.at[0], halo_sem.at[1], (i, left), MESH)

    lane = lax.broadcasted_iota(jnp.int32, (TILE, LANES), 1)
    sub = lax.broadcasted_iota(jnp.int32, (TILE, LANES), 0)
    spare = (lane > width) & (lane <= width + piece)
    upper = sub < TILE // 2
    first = (lane < piece - 1) | (lane == LANES - 1)
    second = lane < 2 * piece - 1

    def there(x, p):
        return pltpu.roll(x, (width + 2 - piece * p) % LANES, 1)

    def back(x, p):
        return pltpu.roll(x, (piece * p - width - 2) % LANES, 1)

    def twelve(a, b):
        turned = pltpu.roll(b, TILE // 2, 0)
        a = jnp.where(spare, jnp.where(upper, there(turned, 0), there(b, 1)), a)
        return a, jnp.where(spare, there(turned, 2), b)[: TILE // 2]

    def sixteen(a, b):
        b = jnp.concatenate([b, b], 0)
        outer = jnp.where(first, back(a, 0), back(b, 2))
        inner = second & jnp.logical_not(first)
        return a, jnp.where(upper, b, jnp.where(inner, back(a, 1), pltpu.roll(outer, TILE // 2, 0)))

    def tiles(x):
        return [x[n * TILE : (n + 1) * TILE] for n in range(x.shape[0] // TILE)]
    zlane = lax.broadcasted_iota(jnp.int32, (deep, LANES), 1)
    base = half_way * (j // half_way)
    far = [half_way - base + n for n in range(half_way)]
    near = [base + lax.rem(j - base + n, half_way) for n in range(1, half_way)]
    waited = set()

    def lanes_of(c):
        return slice(c * LANES, min((c + 1) * LANES, total))

    def prepare(ch):
        for r in order:
            if r not in waited and any(abs(r - r2) < 2 for r2 in pairs[ch]):
                waited.add(r)
                for load in big[r]:
                    load.wait()
        for k in range(levels):
            for c in range(count):
                at = lanes_of(c)
                for side, r in enumerate(pairs[ch]):
                    x = widen(q_v[r, k, :, at])
                    south = widen(q_v[r - 1, k, :, at] if r > 0 else south_r[k, :, at])
                    north = widen(q_v[r + 1, k, :, at] if r < rows - 1 else north_r[k, :, at])
                    c_s = widen(mc_v[r, k : k + 1, at])
                    c_n = widen(mc_v[r + 1, k : k + 1, at] if r < rows - 1 else mcn_r[k : k + 1, at])
                    keep = 1.0 + jnp.minimum(c_s, 0.0) - jnp.maximum(c_n, 0.0)
                    x = keep * x + jnp.maximum(c_s, 0.0) * south - jnp.minimum(c_n, 0.0) * north
                    adv_v[ch, k, c, side * body : (side + 1) * body] = x[:body]
                    low = 2 * body + side * rest
                    adv_v[ch, k, c, low : low + rest] = x[body:]
        for m in range(n_lev):
            x, y = (tiles(lon_block(lambda c: adv_v[ch, k, c], total, width, m)) for k in range(levels))
            for n, carrier in enumerate(x[:4] + y[:2]):
                main_s[m, ch, n * TILE : (n + 1) * TILE] = jnp.where(
                    spare, there(y[2 + n // 3], n % 3), carrier)
            main_s[m, ch, base_row : base_row + TILE], main_s[m, ch, ends] = twelve(x[4], y[4])

    def send(ch):
        for m in far + near:
            main_copy(m, ch).start()
        main_r[pl.ds(j, 1), ch] = main_s[pl.ds(j, 1), ch]

    for load in small[:4]:
        load.wait()
    wide = [widen(specific_air_factor * temp_v[:, k, :] * span_s[k]) for k in range(levels)]
    for m in range(n_lev):
        x, y = (lon_block(lambda c: wide[k][:, c * LANES : (c + 1) * LANES], total, width, m)
                for k in range(levels))
        thick_s[m, :TILE], thick_s[m, TILE:] = twelve(x, y)
    zc = widen(zc_v[...])
    halo = jnp.zeros((deep, LANES), jnp.float32)
    for r in range(rows):
        halo = jnp.where(zlane == r, pltpu.roll(zc[r], r, 1) if r else zc[r], halo)
        z_v[r] = zc[r]
    halo_s[...] = halo
    prepare(0)

    pl.semaphore_wait(barrier, n_lev - 1 + jnp.minimum(i, 1) + jnp.minimum(n_lat - 1 - i, 1))
    @pl.when(has_south)
    def _():
        for copy in south_copies:
            copy.start()

    for m in far:
        thick_copy(m).start()
    for m in far:
        main_copy(m, 0).start()

    @pl.when(has_north)
    def _():
        for copy in north_copies:
            copy.start()

    halo_copy.start()
    for m in near:
        thick_copy(m).start()
    for m in near:
        main_copy(m, 0).start()
    main_r[pl.ds(j, 1), 0] = main_s[pl.ds(j, 1), 0]
    thick_r[pl.ds(j, 1)] = thick_s[pl.ds(j, 1)]

    prepare(1)
    send(1)

    prepare(2)
    send(2)
    for ch in range(3, len(pairs) - 1):
        prepare(ch)
        send(ch)

    for m in range(n_lev):
        @pl.when(j != m)
        def _():
            pltpu.make_async_remote_copy(
                thick_s.at[m], thick_r.at[m], thick_ss.at[m], thick_rs.at[m], (i, m), MESH).wait_recv()
    below = jnp.zeros((rows, LANES), jnp.float32)
    for m in reversed(range(n_lev)):
        below_s[m] = below
        t2 = sixteen(thick_r[m, :TILE], thick_r[m, TILE:])
        for k in reversed(range(levels)):
            t = t2[k]
            full_v[m * levels + k] = t
            dens_v[m * levels + k] = jnp.exp((below + 0.5 * t) * (-1.0 / scale_height))
            below = below + t
    for m in far + near:
        below_copy(m).start()
    below_r[pl.ds(j, 1)] = below_s[pl.ds(j, 1)]

    for load in small[4:]:
        load.wait()
    rate = rate_v[...]
    r0 = lax.broadcasted_iota(jnp.int32, rate.shape, 0)
    r1 = lax.broadcasted_iota(jnp.int32, rate.shape, 1)
    merging = jnp.where(r1 < r0, rate, jnp.where(r1 > r0, -rate, 0.0))

    def place(n):
        tail = n - 2 * body
        side = jnp.where(n < 2 * body, n // body, tail // rest)
        kind = jnp.where(n < 2 * body, n - side * body, body + tail - side * rest)
        return side, jnp.where(n < stack, kind, -1)

    _, kind = place(lax.broadcasted_iota(jnp.int32, (padded, bins), 0))
    pick = jnp.where(kind == lax.broadcasted_iota(jnp.int32, (padded, bins), 1), 1.0, 0.0)
    both = jnp.dot(pick, merging, precision=HIGHEST, preferred_element_type=jnp.float32)
    both = lax.dot_general(both, pick, (((1,), (1,)), ((), ())), precision=HIGHEST,
                           preferred_element_type=jnp.float32)
    side0, _ = place(lax.broadcasted_iota(jnp.int32, (padded, padded), 0))
    side1, _ = place(lax.broadcasted_iota(jnp.int32, (padded, padded), 1))
    both = jnp.where(side0 == side1, both, 0.0)
    high = both.astype(jnp.bfloat16)
    low = (both - high.astype(jnp.float32)).astype(jnp.bfloat16)
    merge_v[...] = jnp.concatenate([high, high, low], 1)

    def column(first, n):
        x = jnp.zeros((TILE, LANES), jnp.float32)
        for s in range(TILE):
            x = jnp.where(sub == s, fall_s[first + s % n], x)
        return x

    fall = [column(f * TILE, TILE) for f in range(full)]
    fall = jnp.concatenate(fall + fall + [column(body, rest)], 0)

    def spread(a, b):
        return jnp.concatenate([
            jnp.broadcast_to(a, (body, LANES)), jnp.broadcast_to(b, (body, LANES)),
            jnp.where(sub < rest, a, b)], 0)

    @pl.when(jnp.logical_not(has_south))
    def _():
        south_r[...] = jnp.zeros_like(south_r)

    @pl.when(jnp.logical_not(has_north))
    def _():
        north_r[...] = jnp.zeros_like(north_r)
        mcn_r[...] = jnp.zeros_like(mcn_r)

    @pl.when(has_south)
    def _():
        for k in range(levels):
            pltpu.make_async_remote_copy(
                q_hbm.at[:, 0, k, :], south_r.at[k], north_ss.at[k], north_rs.at[k], (i - 1, j), MESH).wait_recv()

    @pl.when(has_north)
    def _():
        for k in range(levels):
            pltpu.make_async_remote_copy(
                q_hbm.at[:, 0, k, :], north_r.at[k], south_ss.at[k], south_rs.at[k], (i + 1, j), MESH).wait_recv()
        pltpu.make_async_remote_copy(
            mc_hbm.at[0], mcn_r, south_ss.at[levels], south_rs.at[levels], (i + 1, j), MESH).wait_recv()

    final = len(pairs) - 1
    prepare(final)
    send(final)
    for ch, (r, r2) in enumerate(pairs):
        for k in range(deep):
            t = spread(full_v[k, r : r + 1], full_v[k, r2 : r2 + 1])
            ratio_v[ch, k] = t / (t + fall)

    halo_copy.wait_recv()
    halo = halo_r[...]
    for r in range(rows):
        z_v[r] = jnp.where(zlane == width, pltpu.roll(halo, width - r, 1), z_v[r])

    def collect(ch):
        r, r2 = pairs[ch]
        flow = jnp.zeros((stack, LANES), jnp.float32)
        for group in range(0, n_lev, 2):
            for m in (group, group + 1):
                @pl.when(j != m)
                def _():
                    main_arrival(m, ch).wait_recv()

            moved = []
            ks = range(group * levels, (group + 2) * levels)
            unpacked = []
            for m in (group, group + 1):
                x = tiles(main_r[m, ch, :base_row])
                extra = [jnp.where(first, back(a, 0), jnp.where(second, back(b, 1), back(c, 2)))
                         for a, b, c in (x[:3], x[3:])]
                a, b = sixteen(main_r[m, ch, base_row : base_row + TILE], main_r[m, ch, ends])
                unpacked += [x[:4] + [a], x[4:] + extra + [b]]
            for k in ks:
                summed = jnp.concatenate(unpacked[k - group * levels], 0) + flow
                settled = ratio_v[ch, k] * summed
                flow = summed - settled
                z, z2 = z_v[r, k : k + 1], z_v[r2, k : k + 1]
                up = spread(jnp.maximum(z, 0.0), jnp.maximum(z2, 0.0))
                down = spread(jnp.minimum(z, 0.0), jnp.minimum(z2, 0.0))
                west = up * pltpu.roll(settled, 1, 1) + down * settled
                moved.append(settled + west - pltpu.roll(west, LANES - 1, 1))
            x = jnp.concatenate(moved, 1)
            x = jnp.concatenate([x, jnp.zeros((padded - stack, x.shape[1]), jnp.float32)], 0)
            high = x.astype(jnp.bfloat16)
            low = (x - high.astype(jnp.float32)).astype(jnp.bfloat16)
            coag = jnp.dot(merge_v[...], jnp.concatenate([high, low, high], 0),
                           preferred_element_type=jnp.float32)
            for n, k in enumerate(ks):
                dens = spread(dens_v[k, r : r + 1], dens_v[k, r2 : r2 + 1])
                x = moved[n]
                x = (x + dens * x * coag[:stack, n * LANES : (n + 1) * LANES])[:, :width]
                out_ref[:body, r, k, :] = x[:body]
                out_ref[:body, r2, k, :] = x[body : 2 * body]
                out_ref[body:, r, k, :] = x[2 * body : 2 * body + rest]
                out_ref[body:, r2, k, :] = x[2 * body + rest :]

    for ch in range(final):
        collect(ch)

    for m in range(n_lev):
        @pl.when(j != m)
        def _():
            pltpu.make_async_remote_copy(
                below_s.at[m], below_r.at[m], below_ss.at[m], below_rs.at[m], (i, m), MESH).wait_recv()
    lower = []
    for c in range(count):
        x = jnp.zeros((rows, LANES), jnp.float32)
        for m in range(n_lev):
            begin, end = m * width - c * LANES, (m + 1) * width - c * LANES
            if begin < LANES and end > 0:
                x = jnp.where((lane >= begin) & (lane < end), pltpu.roll(below_r[m], begin % LANES, 1), x)
        lower.append(x)
    below = jnp.concatenate(lower, 1)[:, :total]
    for k in reversed(range(levels)):
        t = specific_air_factor * temp_v[:, k, :] * span_s[k]
        height_ref[:, k, :] = below + 0.5 * t
        below = below + t

    halo_copy.wait_send()
    for m in far + near:
        thick_copy(m).wait_send()
        below_copy(m).wait_send()
        for ch in range(final):
            main_copy(m, ch).wait_send()

    @pl.when(has_south)
    def _():
        for copy in south_copies:
            copy.wait_send()

    @pl.when(has_north)
    def _():
        for copy in north_copies:
            copy.wait_send()

    collect(final)
    for m in far + near:
        main_copy(m, final).wait_send()


def hand_over(dust_ref, height_ref, dust_out, height_out, sem_out):
    pieces = sem_out.shape[0] - 1
    step = dust_ref.shape[0] // pieces
    leave = []
    for p in range(pieces):
        part = pl.ds(p * step, step)
        leave.append(pltpu.make_async_copy(dust_ref.at[part], dust_out.at[part], sem_out.at[p]))
    leave.append(pltpu.make_async_copy(height_ref, height_out, sem_out.at[pieces]))
    for copy in leave:
        copy.start()
    for copy in leave:
        copy.wait()


def solution(mesh):
    n_lat, n_lev = mesh.shape["lat"], mesh.shape["lev"]
    vmem = pl.BlockSpec(memory_space=pltpu.VMEM)
    hbm = pl.BlockSpec(memory_space=pltpu.HBM)

    def on_device(*args):
        bins, rows, levels, total = args[0].shape
        width = total // n_lev
        full, rest = bins // 8, bins % 8
        assert full == 2 and rest == 4 and rows == 8 and levels == 2 and n_lev % 2 == 0
        assert width + 1 + -(-(width + 2) // 3) < LANES
        deep = n_lev * levels
        count = -(-total // LANES)
        chunks = len(row_pairs(rows))
        stack = 2 * bins
        padded = -(-stack // 16) * 16
        f32 = jnp.float32
        main = pltpu.VMEM((n_lev, chunks, 7 * TILE + TILE // 2, LANES), f32)
        thick = pltpu.VMEM((n_lev, rows + TILE // 2, LANES), f32)
        edge = pltpu.VMEM((levels, bins, total), f32)
        tile = pltpu.VMEM((n_lev, rows, LANES), f32)
        halo = pltpu.VMEM((deep, LANES), f32)
        dma = pltpu.SemaphoreType.DMA
        args = [pltpu.with_memory_space_constraint(x, pltpu.HBM) for x in args]
        dust, height = pl.pallas_call(
            functools.partial(kernel, n_lat, n_lev),
            out_shape=(
                pltpu.VMEM((bins, rows, deep, width), f32),
                pltpu.VMEM((rows, levels, total), f32),
            ),
            in_specs=[hbm] * 7,
            out_specs=(vmem, vmem),
            scratch_shapes=[
                pltpu.VMEM((rows, levels, bins, total), f32),
                pltpu.VMEM((rows, levels, total), f32), pltpu.VMEM((rows, levels, total), f32),
                pltpu.SMEM((levels,), f32), pltpu.SMEM((bins,), f32),
                pltpu.VMEM((rows, deep, width), f32), pltpu.VMEM((bins, bins), f32),
                main, main, thick, thick, edge, edge, pltpu.VMEM((levels, total), f32), tile, tile,
                halo, halo,
                pltpu.VMEM((chunks, levels, count, stack, LANES), f32),
                pltpu.VMEM((chunks, deep, stack, LANES), f32),
                pltpu.VMEM((deep, rows, LANES), f32), pltpu.VMEM((deep, rows, LANES), f32),
                pltpu.VMEM((rows, deep, LANES), f32),
                                pltpu.VMEM((padded, 3 * padded), jnp.bfloat16),
                dma((rows * levels,)), dma((6,)),
                dma((n_lev, chunks)), dma((n_lev, chunks)),
                dma((n_lev,)), dma((n_lev,)), dma((n_lev,)), dma((n_lev,)),
                dma((levels,)), dma((levels,)), dma((levels + 1,)), dma((levels + 1,)), dma((2,)),
            ],
            compiler_params=pltpu.CompilerParams(
                collective_id=0, has_side_effects=True, vmem_limit_bytes=32 * 1024 * 1024),
        )(*args)
        return pl.pallas_call(
            hand_over,
            out_shape=(
                jax.ShapeDtypeStruct((bins, rows, deep, width), f32),
                jax.ShapeDtypeStruct(height.shape, f32)),
            in_specs=[vmem, vmem],
            out_specs=(hbm, hbm),
            scratch_shapes=[dma((5,))],
            compiler_params=pltpu.CompilerParams(vmem_limit_bytes=32 * 1024 * 1024),
        )(dust, height)

    in_specs = (
        P(None, "lat", "lev", None),
        P("lat", "lev", None),
        P("lat", "lev", None),
        P("lev"),
        P(),
        P("lat", None, "lev"),
        P(),
    )
    out_specs = (P(None, "lat", None, "lev"), P("lat", "lev", None))
    return jax.shard_map(
        on_device, mesh=mesh, in_specs=in_specs, out_specs=out_specs, check_vma=False
    )
```

```python
import functools

import jax
import jax.numpy as jnp
from jax import lax
from jax.experimental import pallas as pl
from jax.experimental.pallas import tpu as pltpu
from jax.sharding import PartitionSpec as P

specific_air_factor = 0.0293
scale_height = 7.0
LANES = 128
TILE = 8
MESH = pl.DeviceIdType.MESH
HIGHEST = lax.Precision.HIGHEST


def widen(x):
    short = -x.shape[-1] % LANES
    if short:
        x = jnp.concatenate([x, jnp.zeros((*x.shape[:-1], short), x.dtype)], -1)
    return x


def lon_block(tile, total, width, block):
    count = -(-total // LANES)
    last = total % LANES
    start = block * width - 1
    c, off = start // LANES, start % LANES

    def piece(i):
        if i < 0:
            x = tile(count - 1)
            return pltpu.roll(x, (LANES - last) % LANES, x.ndim - 1)
        if i == count:
            return tile(0)
        x = tile(i)
        if i == count - 1 and last and total < start + width + 2:
            lane = lax.broadcasted_iota(jnp.int32, x.shape, x.ndim - 1)
            x = jnp.where(lane < last, x, pltpu.roll(tile(0), last, x.ndim - 1))
        return x

    x = piece(c)
    if off + width + 2 > LANES:
        lane = lax.broadcasted_iota(jnp.int32, x.shape, x.ndim - 1)
        x = jnp.where(lane >= off, x, piece(c + 1))
    return pltpu.roll(x, (2 * LANES - off - 1) % LANES, x.ndim - 1)


def row_pairs(rows):
    return [(r, r + 1) for r in range(1, rows - 1, 2)] + [(0, rows - 1)]


def work_off(width, bins, levels, group, rows_at, packed, flow, ratio, dens, zonal, merge, store):
    stack, body, rest = 2 * bins, bins // TILE * TILE, bins % TILE
    padded = -(-stack // 16) * 16
    piece = -(-(width + 2) // 3)
    base_row, ends = 6 * TILE, slice(7 * TILE, 7 * TILE + TILE // 2)
    lane = lax.broadcasted_iota(jnp.int32, (TILE, LANES), 1)
    sub = lax.broadcasted_iota(jnp.int32, (TILE, LANES), 0)
    near_end = (lane < piece - 1) | (lane == LANES - 1)
    second = lane < 2 * piece - 1
    upper = sub < TILE // 2

    def back(x, p):
        return pltpu.roll(x, (piece * p - width - 2) % LANES, 1)

    def spread(pair):
        a, b = pair
        return jnp.concatenate([
            jnp.broadcast_to(a, (body, LANES)), jnp.broadcast_to(b, (body, LANES)),
            jnp.where(sub < rest, a, b)], 0)

    unpacked = []
    for read in packed:
        y = read(slice(0, base_row))
        x = [y[n * TILE : (n + 1) * TILE] for n in range(6)]
        extra = [jnp.where(near_end, back(a, 0), jnp.where(second, back(b, 1), back(c, 2)))
                 for a, b, c in (x[:3], x[3:])]
        a, b = read(slice(base_row, base_row + TILE)), read(ends)
        b = jnp.concatenate([b, b], 0)
        outer = jnp.where(near_end, back(a, 0), back(b, 2))
        inner = second & jnp.logical_not(near_end)
        b = jnp.where(upper, b, jnp.where(inner, back(a, 1), pltpu.roll(outer, TILE // 2, 0)))
        unpacked += [x[:4] + [a], x[4:] + extra + [b]]
    moved = []
    ks = range(group * levels, (group + len(packed)) * levels)
    for n, k in enumerate(ks):
        summed = jnp.concatenate(unpacked[n], 0) + flow
        settled = ratio(k) * summed
        flow = summed - settled
        up, stay, down = (spread(pair) for pair in zonal(k))
        moved.append(stay * settled + up * pltpu.roll(settled, 1, 1)
                     - down * pltpu.roll(settled, LANES - 1, 1))
    x = jnp.concatenate(moved, 1)
    x = jnp.concatenate([x, jnp.zeros((padded - stack, x.shape[1]), jnp.float32)], 0)
    high = x.astype(jnp.bfloat16)
    low = (x - high.astype(jnp.float32)).astype(jnp.bfloat16)
    coag = jnp.dot(merge[...], jnp.concatenate([high, low, high], 0), preferred_element_type=jnp.float32)
    for n, k in enumerate(ks):
        x = moved[n]
        x = (x + spread(dens(k)) * x * coag[:stack, n * LANES : (n + 1) * LANES])[:, :width]
        for side, at in enumerate(rows_at):
            store[:body, at, k, :] = x[side * body : (side + 1) * body]
            low_end = 2 * body + side * rest
            store[body:, at, k, :] = x[low_end : low_end + rest]
    return flow


def read_rows(ref, r, r2, k):
    return ref[r, k : k + 1], ref[r2, k : k + 1]


def read_levels(ref, r, r2, k):
    return ref[k, r : r + 1], ref[k, r2 : r2 + 1]


def kernel(
    n_lat, n_lev,
    q_hbm, mc_hbm, temp_hbm, span_hbm, fall_hbm, zc_hbm, rate_hbm,
    out_ref, height_ref, pair_ref, flow_ref, late_ref, ratio_v, dens_v, z_v, stay_v, east_v, merge_v,
    q_v, mc_v, temp_v, span_s, fall_s, zc_v, rate_v,
    main_s, main_r, thick_s, thick_r, south_r, north_r, mcn_r, below_s, below_r,
    halo_s, halo_r, adv_v, full_v,
    q_sem, load_sem, main_ss, main_rs, thick_ss, thick_rs,
    below_ss, below_rs, north_ss, north_rs, south_ss, south_rs, halo_sem,
):
    i, j = lax.axis_index("lat"), lax.axis_index("lev")
    rows, levels, bins, total = q_v.shape
    width = total // n_lev
    full = bins // TILE
    rest = bins % TILE
    body = full * TILE
    pairs = row_pairs(rows)
    stack = 2 * bins
    deep = n_lev * levels
    piece = -(-(width + 2) // 3)
    base_row, ends = 6 * TILE, slice(7 * TILE, 7 * TILE + TILE // 2)
    padded = -(-stack // 16) * 16
    count = -(-total // LANES)
    half_way = n_lev // 2
    has_south, has_north = i > 0, i < n_lat - 1
    left = lax.rem(j + n_lev - 1, n_lev)

    barrier = pltpu.get_barrier_semaphore()
    for d in range(1, n_lev):
        pl.semaphore_signal(barrier, inc=1, device_id=(i, lax.rem(j + d, n_lev)), device_id_type=MESH)

    @pl.when(has_south)
    def _():
        pl.semaphore_signal(barrier, inc=1, device_id=(i - 1, j), device_id_type=MESH)

    @pl.when(has_north)
    def _():
        pl.semaphore_signal(barrier, inc=1, device_id=(i + 1, j), device_id_type=MESH)

    small = [
        pltpu.make_async_copy(src, dst, load_sem.at[number])
        for number, (src, dst) in enumerate((
            (span_hbm, span_s), (temp_hbm, temp_v), (mc_hbm, mc_v), (zc_hbm, zc_v),
            (fall_hbm, fall_s), (rate_hbm, rate_v)))
    ]
    big = [[pltpu.make_async_copy(q_hbm.at[:, r, k, :], q_v.at[r, k], q_sem.at[r * levels + k])
            for k in range(levels)] for r in range(rows)]
    for load in small[:4]:
        load.start()
    order = list(dict.fromkeys(
        n for pair in pairs for r in pair for n in (r - 1, r, r + 1) if 0 <= n < rows))
    for r in order:
        for load in big[r]:
            load.start()
    for load in small[4:]:
        load.start()

    def main_copy(m, ch):
        return pltpu.make_async_remote_copy(
            main_s.at[m, ch], main_r.at[j, ch], main_ss.at[m, ch], main_rs.at[j, ch], (i, m), MESH)

    def main_arrival(m, ch):
        return pltpu.make_async_remote_copy(
            main_s.at[m, ch], main_r.at[m, ch], main_ss.at[m, ch], main_rs.at[m, ch], (i, m), MESH)

    def thick_copy(m):
        return pltpu.make_async_remote_copy(
            thick_s.at[m], thick_r.at[j], thick_ss.at[m], thick_rs.at[j], (i, m), MESH)

    def below_copy(m):
        return pltpu.make_async_remote_copy(
            below_s.at[m], below_r.at[j], below_ss.at[m], below_rs.at[j], (i, m), MESH)

    north_copies = [
        pltpu.make_async_remote_copy(
            q_hbm.at[:, rows - 1, k, :], south_r.at[k], north_ss.at[k], north_rs.at[k], (i + 1, j), MESH)
        for k in range(levels)]
    south_copies = [
        pltpu.make_async_remote_copy(
            q_hbm.at[:, 0, k, :], north_r.at[k], south_ss.at[k], south_rs.at[k], (i - 1, j), MESH)
        for k in range(levels)]
    south_copies.append(pltpu.make_async_remote_copy(
        mc_hbm.at[0], mcn_r, south_ss.at[levels], south_rs.at[levels], (i - 1, j), MESH))
    halo_copy = pltpu.make_async_remote_copy(
        halo_s, halo_r, halo_sem.at[0], halo_sem.at[1], (i, left), MESH)

    lane = lax.broadcasted_iota(jnp.int32, (TILE, LANES), 1)
    sub = lax.broadcasted_iota(jnp.int32, (TILE, LANES), 0)
    spare = (lane > width) & (lane <= width + piece)
    upper = sub < TILE // 2
    first = (lane < piece - 1) | (lane == LANES - 1)
    second = lane < 2 * piece - 1

    def there(x, p):
        return pltpu.roll(x, (width + 2 - piece * p) % LANES, 1)

    def back(x, p):
        return pltpu.roll(x, (piece * p - width - 2) % LANES, 1)

    def twelve(a, b):
        turned = pltpu.roll(b, TILE // 2, 0)
        a = jnp.where(spare, jnp.where(upper, there(turned, 0), there(b, 1)), a)
        return a, jnp.where(spare, there(turned, 2), b)[: TILE // 2]

    def sixteen(a, b):
        b = jnp.concatenate([b, b], 0)
        outer = jnp.where(first, back(a, 0), back(b, 2))
        inner = second & jnp.logical_not(first)
        return a, jnp.where(upper, b, jnp.where(inner, back(a, 1), pltpu.roll(outer, TILE // 2, 0)))

    def tiles(x):
        return [x[n * TILE : (n + 1) * TILE] for n in range(x.shape[0] // TILE)]
    zlane = lax.broadcasted_iota(jnp.int32, (deep, LANES), 1)
    base = half_way * (j // half_way)
    far = [half_way - base + n for n in range(half_way)]
    near = [base + lax.rem(j - base + n, half_way) for n in range(1, half_way)]
    waited = set()

    def lanes_of(c):
        return slice(c * LANES, min((c + 1) * LANES, total))

    def prepare(ch):
        for r in order:
            if r not in waited and any(abs(r - r2) < 2 for r2 in pairs[ch]):
                waited.add(r)
                for load in big[r]:
                    load.wait()
        for k in range(levels):
            for c in range(count):
                at = lanes_of(c)
                for side, r in enumerate(pairs[ch]):
                    x = widen(q_v[r, k, :, at])
                    south = widen(q_v[r - 1, k, :, at] if r > 0 else south_r[k, :, at])
                    north = widen(q_v[r + 1, k, :, at] if r < rows - 1 else north_r[k, :, at])
                    c_s = widen(mc_v[r, k : k + 1, at])
                    c_n = widen(mc_v[r + 1, k : k + 1, at] if r < rows - 1 else mcn_r[k : k + 1, at])
                    keep = 1.0 + jnp.minimum(c_s, 0.0) - jnp.maximum(c_n, 0.0)
                    x = keep * x + jnp.maximum(c_s, 0.0) * south - jnp.minimum(c_n, 0.0) * north
                    adv_v[ch, k, c, side * body : (side + 1) * body] = x[:body]
                    low = 2 * body + side * rest
                    adv_v[ch, k, c, low : low + rest] = x[body:]
        for m in range(n_lev):
            x, y = (tiles(lon_block(lambda c: adv_v[ch, k, c], total, width, m)) for k in range(levels))
            for n, carrier in enumerate(x[:4] + y[:2]):
                main_s[m, ch, n * TILE : (n + 1) * TILE] = jnp.where(
                    spare, there(y[2 + n // 3], n % 3), carrier)
            main_s[m, ch, base_row : base_row + TILE], main_s[m, ch, ends] = twelve(x[4], y[4])

    def send(ch):
        for m in far + near:
            main_copy(m, ch).start()
        main_r[pl.ds(j, 1), ch] = main_s[pl.ds(j, 1), ch]

    for load in small[:4]:
        load.wait()
    wide = [widen(specific_air_factor * temp_v[:, k, :] * span_s[k]) for k in range(levels)]
    for m in range(n_lev):
        x, y = (lon_block(lambda c: wide[k][:, c * LANES : (c + 1) * LANES], total, width, m)
                for k in range(levels))
        thick_s[m, :TILE], thick_s[m, TILE:] = twelve(x, y)
    zc = widen(zc_v[...])
    halo = jnp.zeros((deep, LANES), jnp.float32)
    for r in range(rows):
        halo = jnp.where(zlane == r, pltpu.roll(zc[r], r, 1) if r else zc[r], halo)
        z_v[r] = zc[r]
    halo_s[...] = halo
    prepare(0)

    pl.semaphore_wait(barrier, n_lev - 1 + jnp.minimum(i, 1) + jnp.minimum(n_lat - 1 - i, 1))
    @pl.when(has_south)
    def _():
        for copy in south_copies:
            copy.start()

    for m in far:
        thick_copy(m).start()
    for m in far:
        main_copy(m, 0).start()

    @pl.when(has_north)
    def _():
        for copy in north_copies:
            copy.start()

    halo_copy.start()
    for m in near:
        thick_copy(m).start()
    for m in near:
        main_copy(m, 0).start()
    main_r[pl.ds(j, 1), 0] = main_s[pl.ds(j, 1), 0]
    thick_r[pl.ds(j, 1)] = thick_s[pl.ds(j, 1)]

    prepare(1)
    send(1)

    prepare(2)
    send(2)
    for ch in range(3, len(pairs) - 1):
        prepare(ch)
        send(ch)

    for m in range(n_lev):
        @pl.when(j != m)
        def _():
            pltpu.make_async_remote_copy(
                thick_s.at[m], thick_r.at[m], thick_ss.at[m], thick_rs.at[m], (i, m), MESH).wait_recv()
    below = jnp.zeros((rows, LANES), jnp.float32)
    for m in reversed(range(n_lev)):
        below_s[m] = below
        t2 = sixteen(thick_r[m, :TILE], thick_r[m, TILE:])
        for k in reversed(range(levels)):
            t = t2[k]
            full_v[m * levels + k] = t
            dens_v[m * levels + k] = jnp.exp((below + 0.5 * t) * (-1.0 / scale_height))
            below = below + t
    for m in far + near:
        below_copy(m).start()
    below_r[pl.ds(j, 1)] = below_s[pl.ds(j, 1)]

    for load in small[4:]:
        load.wait()
    rate = rate_v[...]
    r0 = lax.broadcasted_iota(jnp.int32, rate.shape, 0)
    r1 = lax.broadcasted_iota(jnp.int32, rate.shape, 1)
    merging = jnp.where(r1 < r0, rate, jnp.where(r1 > r0, -rate, 0.0))

    def place(n):
        tail = n - 2 * body
        side = jnp.where(n < 2 * body, n // body, tail // rest)
        kind = jnp.where(n < 2 * body, n - side * body, body + tail - side * rest)
        return side, jnp.where(n < stack, kind, -1)

    _, kind = place(lax.broadcasted_iota(jnp.int32, (padded, bins), 0))
    pick = jnp.where(kind == lax.broadcasted_iota(jnp.int32, (padded, bins), 1), 1.0, 0.0)
    both = jnp.dot(pick, merging, precision=HIGHEST, preferred_element_type=jnp.float32)
    both = lax.dot_general(both, pick, (((1,), (1,)), ((), ())), precision=HIGHEST,
                           preferred_element_type=jnp.float32)
    side0, _ = place(lax.broadcasted_iota(jnp.int32, (padded, padded), 0))
    side1, _ = place(lax.broadcasted_iota(jnp.int32, (padded, padded), 1))
    both = jnp.where(side0 == side1, both, 0.0)
    high = both.astype(jnp.bfloat16)
    low = (both - high.astype(jnp.float32)).astype(jnp.bfloat16)
    merge_v[...] = jnp.concatenate([high, high, low], 1)

    def column(first, n):
        x = jnp.zeros((TILE, LANES), jnp.float32)
        for s in range(TILE):
            x = jnp.where(sub == s, fall_s[first + s % n], x)
        return x

    fall = [column(f * TILE, TILE) for f in range(full)]
    fall = jnp.concatenate(fall + fall + [column(body, rest)], 0)

    def spread(a, b):
        return jnp.concatenate([
            jnp.broadcast_to(a, (body, LANES)), jnp.broadcast_to(b, (body, LANES)),
            jnp.where(sub < rest, a, b)], 0)

    @pl.when(jnp.logical_not(has_south))
    def _():
        south_r[...] = jnp.zeros_like(south_r)

    @pl.when(jnp.logical_not(has_north))
    def _():
        north_r[...] = jnp.zeros_like(north_r)
        mcn_r[...] = jnp.zeros_like(mcn_r)

    @pl.when(has_south)
    def _():
        for k in range(levels):
            pltpu.make_async_remote_copy(
                q_hbm.at[:, 0, k, :], south_r.at[k], north_ss.at[k], north_rs.at[k], (i - 1, j), MESH).wait_recv()

    @pl.when(has_north)
    def _():
        for k in range(levels):
            pltpu.make_async_remote_copy(
                q_hbm.at[:, 0, k, :], north_r.at[k], south_ss.at[k], south_rs.at[k], (i + 1, j), MESH).wait_recv()
        pltpu.make_async_remote_copy(
            mc_hbm.at[0], mcn_r, south_ss.at[levels], south_rs.at[levels], (i + 1, j), MESH).wait_recv()

    final = len(pairs) - 1
    prepare(final)
    send(final)
    for ch, (r, r2) in enumerate(pairs):
        for k in range(deep):
            t = spread(full_v[k, r : r + 1], full_v[k, r2 : r2 + 1])
            ratio_v[ch, k] = t / (t + fall)

    halo_copy.wait_recv()
    halo = halo_r[...]
    for r in range(rows):
        z = jnp.where(zlane == width, pltpu.roll(halo, width - r, 1), z_v[r])
        up, down = jnp.maximum(z, 0.0), jnp.minimum(z, 0.0)
        z_v[r] = up
        east_v[r] = pltpu.roll(down, LANES - 1, 1)
        stay_v[r] = 1.0 + down - pltpu.roll(up, LANES - 1, 1)

    def collect(ch):
        r, r2 = pairs[ch]
        flow = jnp.zeros((stack, LANES), jnp.float32)
        last = ch == len(pairs) - 1
        for group in range(0, n_lev, 2):
            for m in (group, group + 1):
                @pl.when(j != m)
                def _():
                    main_arrival(m, ch).wait_recv()

            if last and group == n_lev - 2:
                flow_ref[...] = flow
                for m in (group, group + 1):
                    late_ref[m - group] = main_r[m, ch]
            else:
                flow = work_off(
                    width, bins, levels, group, (0, 1) if last else (r, r2),
                    [lambda at, m=m: main_r[m, ch, at] for m in (group, group + 1)], flow,
                    lambda k: ratio_v[ch, k], lambda k: read_levels(dens_v, r, r2, k),
                    lambda k: [read_rows(ref, r, r2, k) for ref in (z_v, stay_v, east_v)],
                    merge_v, pair_ref if last else out_ref)

    for ch in range(final):
        collect(ch)

    for m in range(n_lev):
        @pl.when(j != m)
        def _():
            pltpu.make_async_remote_copy(
                below_s.at[m], below_r.at[m], below_ss.at[m], below_rs.at[m], (i, m), MESH).wait_recv()
    lower = []
    for c in range(count):
        x = jnp.zeros((rows, LANES), jnp.float32)
        for m in range(n_lev):
            begin, end = m * width - c * LANES, (m + 1) * width - c * LANES
            if begin < LANES and end > 0:
                x = jnp.where((lane >= begin) & (lane < end), pltpu.roll(below_r[m], begin % LANES, 1), x)
        lower.append(x)
    below = jnp.concatenate(lower, 1)[:, :total]
    for k in reversed(range(levels)):
        t = specific_air_factor * temp_v[:, k, :] * span_s[k]
        height_ref[:, k, :] = below + 0.5 * t
        below = below + t

    halo_copy.wait_send()
    for m in far + near:
        thick_copy(m).wait_send()
        below_copy(m).wait_send()
        for ch in range(final):
            main_copy(m, ch).wait_send()

    @pl.when(has_south)
    def _():
        for copy in south_copies:
            copy.wait_send()

    @pl.when(has_north)
    def _():
        for copy in north_copies:
            copy.wait_send()

    collect(final)
    for m in far + near:
        main_copy(m, final).wait_send()


def hand_over(
    n_lev, dust_ref, height_ref, pair_ref, flow_ref, late_ref, ratio_v, dens_v, z_v, stay_v, east_v, merge_v,
    dust_out, height_out, pair_v, sem_out,
):
    bins, rows, deep, width = dust_ref.shape
    pairs = row_pairs(rows)
    leave = [pltpu.make_async_copy(dust_ref.at[:, 1 : rows - 1], dust_out.at[:, 1 : rows - 1], sem_out.at[0]),
             pltpu.make_async_copy(height_ref, height_out, sem_out.at[1])]
    for copy in leave:
        copy.start()
    r, r2 = pairs[-1]
    pair_v[...] = pair_ref[...]
    work_off(
        width, bins, deep // n_lev, n_lev - 2, (0, 1),
        [lambda at, m=m: late_ref[m, at] for m in range(2)], flow_ref[...],
        lambda k: ratio_v[len(pairs) - 1, k], lambda k: read_levels(dens_v, r, r2, k),
        lambda k: [read_rows(ref, r, r2, k) for ref in (z_v, stay_v, east_v)], merge_v, pair_v)
    for side, at in enumerate((r, r2)):
        leave.append(pltpu.make_async_copy(pair_v.at[:, side], dust_out.at[:, at], sem_out.at[2 + side]))
        leave[-1].start()
    for copy in leave:
        copy.wait()


def solution(mesh):
    n_lat, n_lev = mesh.shape["lat"], mesh.shape["lev"]
    vmem = pl.BlockSpec(memory_space=pltpu.VMEM)
    hbm = pl.BlockSpec(memory_space=pltpu.HBM)

    def on_device(*args):
        bins, rows, levels, total = args[0].shape
        width = total // n_lev
        full, rest = bins // 8, bins % 8
        assert full == 2 and rest == 4 and rows == 8 and levels == 2 and n_lev % 2 == 0
        assert width + 1 + -(-(width + 2) // 3) < LANES
        deep = n_lev * levels
        count = -(-total // LANES)
        chunks = len(row_pairs(rows))
        stack = 2 * bins
        padded = -(-stack // 16) * 16
        f32 = jnp.float32
        main = pltpu.VMEM((n_lev, chunks, 7 * TILE + TILE // 2, LANES), f32)
        thick = pltpu.VMEM((n_lev, rows + TILE // 2, LANES), f32)
        edge = pltpu.VMEM((levels, bins, total), f32)
        tile = pltpu.VMEM((n_lev, rows, LANES), f32)
        halo = pltpu.VMEM((deep, LANES), f32)
        dma = pltpu.SemaphoreType.DMA
        args = [pltpu.with_memory_space_constraint(x, pltpu.HBM) for x in args]
        outcome = pl.pallas_call(
            functools.partial(kernel, n_lat, n_lev),
            out_shape=(
                pltpu.VMEM((bins, rows, deep, width), f32),
                pltpu.VMEM((rows, levels, total), f32),
                pltpu.VMEM((bins, 2, deep, width), f32),
                pltpu.VMEM((stack, LANES), f32),
                pltpu.VMEM((2, 7 * TILE + TILE // 2, LANES), f32),
                pltpu.VMEM((chunks, deep, stack, LANES), f32),
                pltpu.VMEM((deep, rows, LANES), f32),
                pltpu.VMEM((rows, deep, LANES), f32),
                pltpu.VMEM((rows, deep, LANES), f32),
                pltpu.VMEM((rows, deep, LANES), f32),
                pltpu.VMEM((padded, 3 * padded), jnp.bfloat16),
            ),
            in_specs=[hbm] * 7,
            out_specs=(vmem,) * 11,
            scratch_shapes=[
                pltpu.VMEM((rows, levels, bins, total), f32),
                pltpu.VMEM((rows, levels, total), f32), pltpu.VMEM((rows, levels, total), f32),
                pltpu.SMEM((levels,), f32), pltpu.SMEM((bins,), f32),
                pltpu.VMEM((rows, deep, width), f32), pltpu.VMEM((bins, bins), f32),
                main, main, thick, thick, edge, edge, pltpu.VMEM((levels, total), f32), tile, tile,
                halo, halo,
                pltpu.VMEM((chunks, levels, count, stack, LANES), f32),
                pltpu.VMEM((deep, rows, LANES), f32),
                dma((rows * levels,)), dma((6,)),
                dma((n_lev, chunks)), dma((n_lev, chunks)),
                dma((n_lev,)), dma((n_lev,)), dma((n_lev,)), dma((n_lev,)),
                dma((levels,)), dma((levels,)), dma((levels + 1,)), dma((levels + 1,)), dma((2,)),
            ],
            compiler_params=pltpu.CompilerParams(
                collective_id=0, has_side_effects=True, vmem_limit_bytes=32 * 1024 * 1024),
        )(*args)
        return pl.pallas_call(
            functools.partial(hand_over, n_lev),
            out_shape=(
                jax.ShapeDtypeStruct((bins, rows, deep, width), f32),
                jax.ShapeDtypeStruct((rows, levels, total), f32)),
            in_specs=[vmem] * 11,
            out_specs=(hbm, hbm),
            scratch_shapes=[pltpu.VMEM((bins, 2, deep, width), f32), dma((4,))],
            compiler_params=pltpu.CompilerParams(vmem_limit_bytes=32 * 1024 * 1024),
        )(*outcome)

    in_specs = (
        P(None, "lat", "lev", None),
        P("lat", "lev", None),
        P("lat", "lev", None),
        P("lev"),
        P(),
        P("lat", None, "lev"),
        P(),
    )
    out_specs = (P(None, "lat", None, "lev"), P("lat", "lev", None))
    return jax.shard_map(
        on_device, mesh=mesh, in_specs=in_specs, out_specs=out_specs, check_vma=False
    )
```

```python
import functools

import jax
import jax.numpy as jnp
from jax import lax
from jax.experimental import pallas as pl
from jax.experimental.pallas import tpu as pltpu
from jax.sharding import PartitionSpec as P

specific_air_factor = 0.0293
scale_height = 7.0
LANES = 128
TILE = 8
MESH = pl.DeviceIdType.MESH
HIGHEST = lax.Precision.HIGHEST


def widen(x):
    short = -x.shape[-1] % LANES
    if short:
        x = jnp.concatenate([x, jnp.zeros((*x.shape[:-1], short), x.dtype)], -1)
    return x


def lon_block(tile, total, width, block):
    count = -(-total // LANES)
    last = total % LANES
    start = block * width - 1
    c, off = start // LANES, start % LANES

    def piece(i):
        if i < 0:
            x = tile(count - 1)
            return pltpu.roll(x, (LANES - last) % LANES, x.ndim - 1)
        if i == count:
            return tile(0)
        x = tile(i)
        if i == count - 1 and last and total < start + width + 2:
            lane = lax.broadcasted_iota(jnp.int32, x.shape, x.ndim - 1)
            x = jnp.where(lane < last, x, pltpu.roll(tile(0), last, x.ndim - 1))
        return x

    x = piece(c)
    if off + width + 2 > LANES:
        lane = lax.broadcasted_iota(jnp.int32, x.shape, x.ndim - 1)
        x = jnp.where(lane >= off, x, piece(c + 1))
    return pltpu.roll(x, (2 * LANES - off - 1) % LANES, x.ndim - 1)


def row_pairs(rows):
    return [(r, r + 1) for r in range(1, rows - 1, 2)] + [(0, rows - 1)]


def work_off(width, bins, levels, group, rows_at, packed, flow, ratio, dens, zonal, merge, store):
    stack, body, rest = 2 * bins, bins // TILE * TILE, bins % TILE
    padded = -(-stack // 16) * 16
    piece = -(-(width + 2) // 3)
    base_row, ends = 6 * TILE, slice(7 * TILE, 7 * TILE + TILE // 2)
    lane = lax.broadcasted_iota(jnp.int32, (TILE, LANES), 1)
    sub = lax.broadcasted_iota(jnp.int32, (TILE, LANES), 0)
    near_end = (lane < piece - 1) | (lane == LANES - 1)
    second = lane < 2 * piece - 1
    upper = sub < TILE // 2

    def back(x, p):
        return pltpu.roll(x, (piece * p - width - 2) % LANES, 1)

    def spread(pair):
        a, b = pair
        return jnp.concatenate([
            jnp.broadcast_to(a, (body, LANES)), jnp.broadcast_to(b, (body, LANES)),
            jnp.where(sub < rest, a, b)], 0)

    unpacked = []
    for read in packed:
        y = read(slice(0, base_row))
        x = [y[n * TILE : (n + 1) * TILE] for n in range(6)]
        extra = [jnp.where(near_end, back(a, 0), jnp.where(second, back(b, 1), back(c, 2)))
                 for a, b, c in (x[:3], x[3:])]
        a, b = read(slice(base_row, base_row + TILE)), read(ends)
        b = jnp.concatenate([b, b], 0)
        outer = jnp.where(near_end, back(a, 0), back(b, 2))
        inner = second & jnp.logical_not(near_end)
        b = jnp.where(upper, b, jnp.where(inner, back(a, 1), pltpu.roll(outer, TILE // 2, 0)))
        unpacked += [x[:4] + [a], x[4:] + extra + [b]]
    moved = []
    ks = range(group * levels, (group + len(packed)) * levels)
    for n, k in enumerate(ks):
        summed = jnp.concatenate(unpacked[n], 0) + flow
        settled = ratio(k) * summed
        flow = summed - settled
        up, stay, down = (spread(pair) for pair in zonal(k))
        moved.append(stay * settled + up * pltpu.roll(settled, 1, 1)
                     - down * pltpu.roll(settled, LANES - 1, 1))
    x = jnp.concatenate(moved, 1)
    x = jnp.concatenate([x, jnp.zeros((padded - stack, x.shape[1]), jnp.float32)], 0)
    high = x.astype(jnp.bfloat16)
    low = (x - high.astype(jnp.float32)).astype(jnp.bfloat16)
    coag = jnp.dot(merge[...], jnp.concatenate([high, low, high], 0), preferred_element_type=jnp.float32)
    for n, k in enumerate(ks):
        x = moved[n]
        x = (x + spread(dens(k)) * x * coag[:stack, n * LANES : (n + 1) * LANES])[:, :width]
        for side, at in enumerate(rows_at):
            store[:body, at, k, :] = x[side * body : (side + 1) * body]
            low_end = 2 * body + side * rest
            store[body:, at, k, :] = x[low_end : low_end + rest]
    return flow


def read_rows(ref, r, r2, k):
    return ref[r, k : k + 1], ref[r2, k : k + 1]


def read_levels(ref, r, r2, k):
    return ref[k, r : r + 1], ref[k, r2 : r2 + 1]


def kernel(
    n_lat, n_lev,
    q_hbm, mc_hbm, temp_hbm, span_hbm, fall_hbm, zc_hbm, rate_hbm,
    out_ref, height_ref, pair_ref, flow_ref, late_ref, ratio_v, dens_v, z_v, stay_v, east_v, merge_v,
    q_v, mc_v, temp_v, span_s, fall_s, zc_v, rate_v,
    main_s, main_r, thick_s, thick_r, south_r, north_r, mcn_r, below_s, below_r,
    halo_s, halo_r, adv_v, full_v,
    q_sem, load_sem, main_ss, main_rs, thick_ss, thick_rs,
    below_ss, below_rs, north_ss, north_rs, south_ss, south_rs, halo_sem,
):
    i, j = lax.axis_index("lat"), lax.axis_index("lev")
    rows, levels, bins, total = q_v.shape
    width = total // n_lev
    full = bins // TILE
    rest = bins % TILE
    body = full * TILE
    pairs = row_pairs(rows)
    stack = 2 * bins
    deep = n_lev * levels
    piece = -(-(width + 2) // 3)
    base_row, ends = 6 * TILE, slice(7 * TILE, 7 * TILE + TILE // 2)
    padded = -(-stack // 16) * 16
    count = -(-total // LANES)
    half_way = n_lev // 2
    has_south, has_north = i > 0, i < n_lat - 1
    left = lax.rem(j + n_lev - 1, n_lev)

    barrier = pltpu.get_barrier_semaphore()
    for d in range(1, n_lev):
        pl.semaphore_signal(barrier, inc=1, device_id=(i, lax.rem(j + d, n_lev)), device_id_type=MESH)

    @pl.when(has_south)
    def _():
        pl.semaphore_signal(barrier, inc=1, device_id=(i - 1, j), device_id_type=MESH)

    @pl.when(has_north)
    def _():
        pl.semaphore_signal(barrier, inc=1, device_id=(i + 1, j), device_id_type=MESH)

    small = [
        pltpu.make_async_copy(src, dst, load_sem.at[number])
        for number, (src, dst) in enumerate((
            (span_hbm, span_s), (temp_hbm, temp_v), (mc_hbm, mc_v), (zc_hbm, zc_v),
            (fall_hbm, fall_s), (rate_hbm, rate_v)))
    ]
    big = [[pltpu.make_async_copy(q_hbm.at[:, r, k, :], q_v.at[r, k], q_sem.at[r * levels + k])
            for k in range(levels)] for r in range(rows)]
    for load in small[:4]:
        load.start()
    order = list(dict.fromkeys(
        n for pair in pairs for r in pair for n in (r - 1, r, r + 1) if 0 <= n < rows))
    for r in order:
        for load in big[r]:
            load.start()
    for load in small[4:]:
        load.start()

    def main_copy(m, ch):
        return pltpu.make_async_remote_copy(
            main_s.at[m, ch], main_r.at[j, ch], main_ss.at[m, ch], main_rs.at[j, ch], (i, m), MESH)

    def main_arrival(m, ch):
        return pltpu.make_async_remote_copy(
            main_s.at[m, ch], main_r.at[m, ch], main_ss.at[m, ch], main_rs.at[m, ch], (i, m), MESH)

    def thick_copy(m):
        return pltpu.make_async_remote_copy(
            thick_s.at[m], thick_r.at[j], thick_ss.at[m], thick_rs.at[j], (i, m), MESH)

    def below_copy(m):
        return pltpu.make_async_remote_copy(
            below_s.at[m], below_r.at[j], below_ss.at[m], below_rs.at[j], (i, m), MESH)

    north_copies = [
        pltpu.make_async_remote_copy(
            q_hbm.at[:, rows - 1, k, :], south_r.at[k], north_ss.at[k], north_rs.at[k], (i + 1, j), MESH)
        for k in range(levels)]
    south_copies = [
        pltpu.make_async_remote_copy(
            q_hbm.at[:, 0, k, :], north_r.at[k], south_ss.at[k], south_rs.at[k], (i - 1, j), MESH)
        for k in range(levels)]
    south_copies.append(pltpu.make_async_remote_copy(
        mc_hbm.at[0], mcn_r, south_ss.at[levels], south_rs.at[levels], (i - 1, j), MESH))
    halo_copy = pltpu.make_async_remote_copy(
        halo_s, halo_r, halo_sem.at[0], halo_sem.at[1], (i, left), MESH)

    lane = lax.broadcasted_iota(jnp.int32, (TILE, LANES), 1)
    sub = lax.broadcasted_iota(jnp.int32, (TILE, LANES), 0)
    spare = (lane > width) & (lane <= width + piece)
    upper = sub < TILE // 2
    first = (lane < piece - 1) | (lane == LANES - 1)
    second = lane < 2 * piece - 1

    def there(x, p):
        return pltpu.roll(x, (width + 2 - piece * p) % LANES, 1)

    def back(x, p):
        return pltpu.roll(x, (piece * p - width - 2) % LANES, 1)

    def twelve(a, b):
        turned = pltpu.roll(b, TILE // 2, 0)
        a = jnp.where(spare, jnp.where(upper, there(turned, 0), there(b, 1)), a)
        return a, jnp.where(spare, there(turned, 2), b)[: TILE // 2]

    def sixteen(a, b):
        b = jnp.concatenate([b, b], 0)
        outer = jnp.where(first, back(a, 0), back(b, 2))
        inner = second & jnp.logical_not(first)
        return a, jnp.where(upper, b, jnp.where(inner, back(a, 1), pltpu.roll(outer, TILE // 2, 0)))

    def tiles(x):
        return [x[n * TILE : (n + 1) * TILE] for n in range(x.shape[0] // TILE)]
    zlane = lax.broadcasted_iota(jnp.int32, (deep, LANES), 1)
    base = half_way * (j // half_way)
    far = [half_way - base + n for n in range(half_way)]
    near = [base + lax.rem(j - base + n, half_way) for n in range(1, half_way)]
    waited = set()

    def lanes_of(c):
        return slice(c * LANES, min((c + 1) * LANES, total))

    def prepare(ch):
        for r in order:
            if r not in waited and any(abs(r - r2) < 2 for r2 in pairs[ch]):
                waited.add(r)
                for load in big[r]:
                    load.wait()
        for k in range(levels):
            for c in range(count):
                at = lanes_of(c)
                for side, r in enumerate(pairs[ch]):
                    x = widen(q_v[r, k, :, at])
                    south = widen(q_v[r - 1, k, :, at] if r > 0 else south_r[k, :, at])
                    north = widen(q_v[r + 1, k, :, at] if r < rows - 1 else north_r[k, :, at])
                    c_s = widen(mc_v[r, k : k + 1, at])
                    c_n = widen(mc_v[r + 1, k : k + 1, at] if r < rows - 1 else mcn_r[k : k + 1, at])
                    keep = 1.0 + jnp.minimum(c_s, 0.0) - jnp.maximum(c_n, 0.0)
                    x = keep * x + jnp.maximum(c_s, 0.0) * south - jnp.minimum(c_n, 0.0) * north
                    adv_v[ch, k, c, side * body : (side + 1) * body] = x[:body]
                    low = 2 * body + side * rest
                    adv_v[ch, k, c, low : low + rest] = x[body:]
        for m in range(n_lev):
            x, y = (tiles(lon_block(lambda c: adv_v[ch, k, c], total, width, m)) for k in range(levels))
            for n, carrier in enumerate(x[:4] + y[:2]):
                main_s[m, ch, n * TILE : (n + 1) * TILE] = jnp.where(
                    spare, there(y[2 + n // 3], n % 3), carrier)
            main_s[m, ch, base_row : base_row + TILE], main_s[m, ch, ends] = twelve(x[4], y[4])

    def send(ch):
        for m in far + near:
            main_copy(m, ch).start()
        main_r[pl.ds(j, 1), ch] = main_s[pl.ds(j, 1), ch]

    for load in small[:4]:
        load.wait()
    wide = [widen(specific_air_factor * temp_v[:, k, :] * span_s[k]) for k in range(levels)]
    for m in range(n_lev):
        x, y = (lon_block(lambda c: wide[k][:, c * LANES : (c + 1) * LANES], total, width, m)
                for k in range(levels))
        thick_s[m, :TILE], thick_s[m, TILE:] = twelve(x, y)
    zc = widen(zc_v[...])
    halo = jnp.zeros((deep, LANES), jnp.float32)
    for r in range(rows):
        halo = jnp.where(zlane == r, pltpu.roll(zc[r], r, 1) if r else zc[r], halo)
        z_v[r] = zc[r]
    halo_s[...] = halo
    prepare(0)

    pl.semaphore_wait(barrier, n_lev - 1 + jnp.minimum(i, 1) + jnp.minimum(n_lat - 1 - i, 1))
    @pl.when(has_south)
    def _():
        for copy in south_copies:
            copy.start()

    for m in far:
        thick_copy(m).start()
    for m in far:
        main_copy(m, 0).start()

    @pl.when(has_north)
    def _():
        for copy in north_copies:
            copy.start()

    halo_copy.start()
    for m in near:
        thick_copy(m).start()
    for m in near:
        main_copy(m, 0).start()
    main_r[pl.ds(j, 1), 0] = main_s[pl.ds(j, 1), 0]
    thick_r[pl.ds(j, 1)] = thick_s[pl.ds(j, 1)]

    prepare(1)
    send(1)

    prepare(2)
    send(2)
    for ch in range(3, len(pairs) - 1):
        prepare(ch)
        send(ch)

    for m in range(n_lev):
        @pl.when(j != m)
        def _():
            pltpu.make_async_remote_copy(
                thick_s.at[m], thick_r.at[m], thick_ss.at[m], thick_rs.at[m], (i, m), MESH).wait_recv()
    below = jnp.zeros((rows, LANES), jnp.float32)
    for m in reversed(range(n_lev)):
        below_s[m] = below
        t2 = sixteen(thick_r[m, :TILE], thick_r[m, TILE:])
        for k in reversed(range(levels)):
            t = t2[k]
            full_v[m * levels + k] = t
            dens_v[m * levels + k] = jnp.exp((below + 0.5 * t) * (-1.0 / scale_height))
            below = below + t
    for m in far + near:
        below_copy(m).start()
    below_r[pl.ds(j, 1)] = below_s[pl.ds(j, 1)]

    def spread(a, b):
        return jnp.concatenate([
            jnp.broadcast_to(a, (body, LANES)), jnp.broadcast_to(b, (body, LANES)),
            jnp.where(sub < rest, a, b)], 0)

    def ready():
        for load in small[4:]:
            load.wait()
        rate = rate_v[...]
        r0 = lax.broadcasted_iota(jnp.int32, rate.shape, 0)
        r1 = lax.broadcasted_iota(jnp.int32, rate.shape, 1)
        merging = jnp.where(r1 < r0, rate, jnp.where(r1 > r0, -rate, 0.0))

        def place(n):
            tail = n - 2 * body
            side = jnp.where(n < 2 * body, n // body, tail // rest)
            kind = jnp.where(n < 2 * body, n - side * body, body + tail - side * rest)
            return side, jnp.where(n < stack, kind, -1)

        _, kind = place(lax.broadcasted_iota(jnp.int32, (padded, bins), 0))
        pick = jnp.where(kind == lax.broadcasted_iota(jnp.int32, (padded, bins), 1), 1.0, 0.0)
        both = jnp.dot(pick, merging, precision=HIGHEST, preferred_element_type=jnp.float32)
        both = lax.dot_general(both, pick, (((1,), (1,)), ((), ())), precision=HIGHEST,
                               preferred_element_type=jnp.float32)
        side0, _ = place(lax.broadcasted_iota(jnp.int32, (padded, padded), 0))
        side1, _ = place(lax.broadcasted_iota(jnp.int32, (padded, padded), 1))
        both = jnp.where(side0 == side1, both, 0.0)
        high = both.astype(jnp.bfloat16)
        low = (both - high.astype(jnp.float32)).astype(jnp.bfloat16)
        merge_v[...] = jnp.concatenate([high, high, low], 1)

        def column(first, n):
            x = jnp.zeros((TILE, LANES), jnp.float32)
            for s in range(TILE):
                x = jnp.where(sub == s, fall_s[first + s % n], x)
            return x

        fall = [column(f * TILE, TILE) for f in range(full)]
        fall = jnp.concatenate(fall + fall + [column(body, rest)], 0)

        for ch, (r, r2) in enumerate(pairs):
            for k in range(deep):
                t = spread(full_v[k, r : r + 1], full_v[k, r2 : r2 + 1])
                ratio_v[ch, k] = t / (t + fall)

        halo_copy.wait_recv()
        halo = halo_r[...]
        for r in range(rows):
            z = jnp.where(zlane == width, pltpu.roll(halo, width - r, 1), z_v[r])
            up, down = jnp.maximum(z, 0.0), jnp.minimum(z, 0.0)
            z_v[r] = up
            east_v[r] = pltpu.roll(down, LANES - 1, 1)
            stay_v[r] = 1.0 + down - pltpu.roll(up, LANES - 1, 1)


    def collect(ch):
        r, r2 = pairs[ch]
        flow = jnp.zeros((stack, LANES), jnp.float32)
        last = ch == len(pairs) - 1
        for group in range(0, n_lev, 2):
            for m in (group, group + 1):
                @pl.when(j != m)
                def _():
                    main_arrival(m, ch).wait_recv()

            if last and group == n_lev - 2:
                flow_ref[...] = flow
                for m in (group, group + 1):
                    late_ref[m - group] = main_r[m, ch]
            else:
                flow = work_off(
                    width, bins, levels, group, (0, 1) if last else (r, r2),
                    [lambda at, m=m: main_r[m, ch, at] for m in (group, group + 1)], flow,
                    lambda k: ratio_v[ch, k], lambda k: read_levels(dens_v, r, r2, k),
                    lambda k: [read_rows(ref, r, r2, k) for ref in (z_v, stay_v, east_v)],
                    merge_v, pair_ref if last else out_ref)

    @pl.when(j < half_way)
    def _():
        ready()
        collect(0)

    @pl.when(jnp.logical_not(has_south))
    def _():
        south_r[...] = jnp.zeros_like(south_r)

    @pl.when(jnp.logical_not(has_north))
    def _():
        north_r[...] = jnp.zeros_like(north_r)
        mcn_r[...] = jnp.zeros_like(mcn_r)

    @pl.when(has_south)
    def _():
        for k in range(levels):
            pltpu.make_async_remote_copy(
                q_hbm.at[:, 0, k, :], south_r.at[k], north_ss.at[k], north_rs.at[k], (i - 1, j), MESH).wait_recv()

    @pl.when(has_north)
    def _():
        for k in range(levels):
            pltpu.make_async_remote_copy(
                q_hbm.at[:, 0, k, :], north_r.at[k], south_ss.at[k], south_rs.at[k], (i + 1, j), MESH).wait_recv()
        pltpu.make_async_remote_copy(
            mc_hbm.at[0], mcn_r, south_ss.at[levels], south_rs.at[levels], (i + 1, j), MESH).wait_recv()

    final = len(pairs) - 1
    prepare(final)
    send(final)

    @pl.when(j >= half_way)
    def _():
        ready()
        collect(0)

    for ch in range(1, final):
        collect(ch)

    for m in range(n_lev):
        @pl.when(j != m)
        def _():
            pltpu.make_async_remote_copy(
                below_s.at[m], below_r.at[m], below_ss.at[m], below_rs.at[m], (i, m), MESH).wait_recv()
    lower = []
    for c in range(count):
        x = jnp.zeros((rows, LANES), jnp.float32)
        for m in range(n_lev):
            begin, end = m * width - c * LANES, (m + 1) * width - c * LANES
            if begin < LANES and end > 0:
                x = jnp.where((lane >= begin) & (lane < end), pltpu.roll(below_r[m], begin % LANES, 1), x)
        lower.append(x)
    below = jnp.concatenate(lower, 1)[:, :total]
    for k in reversed(range(levels)):
        t = specific_air_factor * temp_v[:, k, :] * span_s[k]
        height_ref[:, k, :] = below + 0.5 * t
        below = below + t

    halo_copy.wait_send()
    for m in far + near:
        thick_copy(m).wait_send()
        below_copy(m).wait_send()
        for ch in range(final):
            main_copy(m, ch).wait_send()

    @pl.when(has_south)
    def _():
        for copy in south_copies:
            copy.wait_send()

    @pl.when(has_north)
    def _():
        for copy in north_copies:
            copy.wait_send()

    collect(final)
    for m in far + near:
        main_copy(m, final).wait_send()


def hand_over(
    n_lev, dust_ref, height_ref, pair_ref, flow_ref, late_ref, ratio_v, dens_v, z_v, stay_v, east_v, merge_v,
    dust_out, height_out, pair_v, sem_out,
):
    bins, rows, deep, width = dust_ref.shape
    pairs = row_pairs(rows)
    leave = [pltpu.make_async_copy(dust_ref.at[:, 1 : rows - 1], dust_out.at[:, 1 : rows - 1], sem_out.at[0]),
             pltpu.make_async_copy(height_ref, height_out, sem_out.at[1])]
    r, r2 = pairs[-1]
    done = deep - 2 * (deep // n_lev)
    for side, at in enumerate((r, r2)):
        leave.append(pltpu.make_async_copy(
            pair_ref.at[:, side, :done], dust_out.at[:, at, :done], sem_out.at[4 + side]))
    for copy in leave:
        copy.start()
    work_off(
        width, bins, deep // n_lev, n_lev - 2, (0, 1),
        [lambda at, m=m: late_ref[m, at] for m in range(2)], flow_ref[...],
        lambda k: ratio_v[len(pairs) - 1, k], lambda k: read_levels(dens_v, r, r2, k),
        lambda k: [read_rows(ref, r, r2, k) for ref in (z_v, stay_v, east_v)], merge_v, pair_v)
    for side, at in enumerate((r, r2)):
        leave.append(pltpu.make_async_copy(
            pair_v.at[:, side, done:], dust_out.at[:, at, done:], sem_out.at[2 + side]))
        leave[-1].start()
    for copy in leave:
        copy.wait()


def solution(mesh):
    n_lat, n_lev = mesh.shape["lat"], mesh.shape["lev"]
    vmem = pl.BlockSpec(memory_space=pltpu.VMEM)
    hbm = pl.BlockSpec(memory_space=pltpu.HBM)

    def on_device(*args):
        bins, rows, levels, total = args[0].shape
        width = total // n_lev
        full, rest = bins // 8, bins % 8
        assert full == 2 and rest == 4 and rows == 8 and levels == 2 and n_lev % 2 == 0
        assert width + 1 + -(-(width + 2) // 3) < LANES
        deep = n_lev * levels
        count = -(-total // LANES)
        chunks = len(row_pairs(rows))
        stack = 2 * bins
        padded = -(-stack // 16) * 16
        f32 = jnp.float32
        main = pltpu.VMEM((n_lev, chunks, 7 * TILE + TILE // 2, LANES), f32)
        thick = pltpu.VMEM((n_lev, rows + TILE // 2, LANES), f32)
        edge = pltpu.VMEM((levels, bins, total), f32)
        tile = pltpu.VMEM((n_lev, rows, LANES), f32)
        halo = pltpu.VMEM((deep, LANES), f32)
        dma = pltpu.SemaphoreType.DMA
        args = [pltpu.with_memory_space_constraint(x, pltpu.HBM) for x in args]
        outcome = pl.pallas_call(
            functools.partial(kernel, n_lat, n_lev),
            out_shape=(
                pltpu.VMEM((bins, rows, deep, width), f32),
                pltpu.VMEM((rows, levels, total), f32),
                pltpu.VMEM((bins, 2, deep, width), f32),
                pltpu.VMEM((stack, LANES), f32),
                pltpu.VMEM((2, 7 * TILE + TILE // 2, LANES), f32),
                pltpu.VMEM((chunks, deep, stack, LANES), f32),
                pltpu.VMEM((deep, rows, LANES), f32),
                pltpu.VMEM((rows, deep, LANES), f32),
                pltpu.VMEM((rows, deep, LANES), f32),
                pltpu.VMEM((rows, deep, LANES), f32),
                pltpu.VMEM((padded, 3 * padded), jnp.bfloat16),
            ),
            in_specs=[hbm] * 7,
            out_specs=(vmem,) * 11,
            scratch_shapes=[
                pltpu.VMEM((rows, levels, bins, total), f32),
                pltpu.VMEM((rows, levels, total), f32), pltpu.VMEM((rows, levels, total), f32),
                pltpu.SMEM((levels,), f32), pltpu.SMEM((bins,), f32),
                pltpu.VMEM((rows, deep, width), f32), pltpu.VMEM((bins, bins), f32),
                main, main, thick, thick, edge, edge, pltpu.VMEM((levels, total), f32), tile, tile,
                halo, halo,
                pltpu.VMEM((chunks, levels, count, stack, LANES), f32),
                pltpu.VMEM((deep, rows, LANES), f32),
                dma((rows * levels,)), dma((6,)),
                dma((n_lev, chunks)), dma((n_lev, chunks)),
                dma((n_lev,)), dma((n_lev,)), dma((n_lev,)), dma((n_lev,)),
                dma((levels,)), dma((levels,)), dma((levels + 1,)), dma((levels + 1,)), dma((2,)),
            ],
            compiler_params=pltpu.CompilerParams(
                collective_id=0, has_side_effects=True, vmem_limit_bytes=32 * 1024 * 1024),
        )(*args)
        return pl.pallas_call(
            functools.partial(hand_over, n_lev),
            out_shape=(
                jax.ShapeDtypeStruct((bins, rows, deep, width), f32),
                jax.ShapeDtypeStruct((rows, levels, total), f32)),
            in_specs=[vmem] * 11,
            out_specs=(hbm, hbm),
            scratch_shapes=[pltpu.VMEM((bins, 2, deep, width), f32), dma((6,))],
            compiler_params=pltpu.CompilerParams(vmem_limit_bytes=32 * 1024 * 1024),
        )(*outcome)

    in_specs = (
        P(None, "lat", "lev", None),
        P("lat", "lev", None),
        P("lat", "lev", None),
        P("lev"),
        P(),
        P("lat", None, "lev"),
        P(),
    )
    out_specs = (P(None, "lat", None, "lev"), P("lat", "lev", None))
    return jax.shard_map(
        on_device, mesh=mesh, in_specs=in_specs, out_specs=out_specs, check_vma=False
    )
```

```python
import functools

import jax
import jax.numpy as jnp
from jax import lax
from jax.experimental import pallas as pl
from jax.experimental.pallas import tpu as pltpu
from jax.sharding import PartitionSpec as P

specific_air_factor = 0.0293
scale_height = 7.0
LANES = 128
TILE = 8
MESH = pl.DeviceIdType.MESH
HIGHEST = lax.Precision.HIGHEST


def widen(x):
    short = -x.shape[-1] % LANES
    if short:
        x = jnp.concatenate([x, jnp.zeros((*x.shape[:-1], short), x.dtype)], -1)
    return x


def lon_block(tile, total, width, block):
    count = -(-total // LANES)
    last = total % LANES
    start = block * width - 1
    c, off = start // LANES, start % LANES

    def piece(i):
        if i < 0:
            x = tile(count - 1)
            return pltpu.roll(x, (LANES - last) % LANES, x.ndim - 1)
        if i == count:
            return tile(0)
        x = tile(i)
        if i == count - 1 and last and total < start + width + 2:
            lane = lax.broadcasted_iota(jnp.int32, x.shape, x.ndim - 1)
            x = jnp.where(lane < last, x, pltpu.roll(tile(0), last, x.ndim - 1))
        return x

    x = piece(c)
    if off + width + 2 > LANES:
        lane = lax.broadcasted_iota(jnp.int32, x.shape, x.ndim - 1)
        x = jnp.where(lane >= off, x, piece(c + 1))
    return pltpu.roll(x, (2 * LANES - off - 1) % LANES, x.ndim - 1)


def row_pairs(rows):
    return [(r, r + 1) for r in range(1, rows - 1, 2)] + [(0, rows - 1)]


def work_off(width, bins, levels, group, rows_at, packed, flow, ratio, dens, zonal, merge, store):
    stack, body, rest = 2 * bins, bins // TILE * TILE, bins % TILE
    padded = -(-stack // 16) * 16
    piece = -(-(width + 2) // 3)
    base_row, ends = 6 * TILE, slice(7 * TILE, 7 * TILE + TILE // 2)
    lane = lax.broadcasted_iota(jnp.int32, (TILE, LANES), 1)
    sub = lax.broadcasted_iota(jnp.int32, (TILE, LANES), 0)
    near_end = (lane < piece - 1) | (lane == LANES - 1)
    second = lane < 2 * piece - 1
    upper = sub < TILE // 2

    def back(x, p):
        return pltpu.roll(x, (piece * p - width - 2) % LANES, 1)

    def spread(pair):
        a, b = pair
        return jnp.concatenate([
            jnp.broadcast_to(a, (body, LANES)), jnp.broadcast_to(b, (body, LANES)),
            jnp.where(sub < rest, a, b)], 0)

    unpacked = []
    for read in packed:
        y = read(slice(0, base_row))
        x = [y[n * TILE : (n + 1) * TILE] for n in range(6)]
        extra = [jnp.where(near_end, back(a, 0), jnp.where(second, back(b, 1), back(c, 2)))
                 for a, b, c in (x[:3], x[3:])]
        a, b = read(slice(base_row, base_row + TILE)), read(ends)
        b = jnp.concatenate([b, b], 0)
        outer = jnp.where(near_end, back(a, 0), back(b, 2))
        inner = second & jnp.logical_not(near_end)
        b = jnp.where(upper, b, jnp.where(inner, back(a, 1), pltpu.roll(outer, TILE // 2, 0)))
        unpacked += [x[:4] + [a], x[4:] + extra + [b]]
    moved = []
    ks = range(group * levels, (group + len(packed)) * levels)
    for n, k in enumerate(ks):
        summed = jnp.concatenate(unpacked[n], 0) + flow
        settled = ratio(k) * summed
        flow = summed - settled
        up, stay, down = (spread(pair) for pair in zonal(k))
        moved.append(stay * settled + up * pltpu.roll(settled, 1, 1)
                     - down * pltpu.roll(settled, LANES - 1, 1))
    x = jnp.concatenate(moved, 1)
    x = jnp.concatenate([x, jnp.zeros((padded - stack, x.shape[1]), jnp.float32)], 0)
    high = x.astype(jnp.bfloat16)
    low = (x - high.astype(jnp.float32)).astype(jnp.bfloat16)
    coag = jnp.dot(merge[...], jnp.concatenate([high, low, high], 0), preferred_element_type=jnp.float32)
    for n, k in enumerate(ks):
        x = moved[n]
        x = (x + spread(dens(k)) * x * coag[:stack, n * LANES : (n + 1) * LANES])[:, :width]
        for side, at in enumerate(rows_at):
            store[:body, at, k, :] = x[side * body : (side + 1) * body]
            low_end = 2 * body + side * rest
            store[body:, at, k, :] = x[low_end : low_end + rest]
    return flow


def read_rows(ref, r, r2, k):
    return ref[r, k : k + 1], ref[r2, k : k + 1]


def read_levels(ref, r, r2, k):
    return ref[k, r : r + 1], ref[k, r2 : r2 + 1]


def kernel(
    n_lat, n_lev,
    q_hbm, mc_hbm, temp_hbm, span_hbm, fall_hbm, zc_hbm, rate_hbm,
    out_ref, height_ref, pair_ref, flow_ref, late_ref, ratio_v, dens_v, z_v, stay_v, east_v, merge_v,
    q_v, mc_v, temp_v, span_s, fall_s, zc_v, rate_v,
    main_s, main_r, thick_s, thick_r, south_r, north_r, mcn_r, below_s, below_r,
    halo_s, halo_r, adv_v, full_v,
    q_sem, load_sem, main_ss, main_rs, thick_ss, thick_rs,
    below_ss, below_rs, north_ss, north_rs, south_ss, south_rs, halo_sem,
):
    i, j = lax.axis_index("lat"), lax.axis_index("lev")
    rows, levels, bins, total = q_v.shape
    width = total // n_lev
    full = bins // TILE
    rest = bins % TILE
    body = full * TILE
    pairs = row_pairs(rows)
    stack = 2 * bins
    deep = n_lev * levels
    piece = -(-(width + 2) // 3)
    base_row, ends = 6 * TILE, slice(7 * TILE, 7 * TILE + TILE // 2)
    padded = -(-stack // 16) * 16
    count = -(-total // LANES)
    half_way = n_lev // 2
    has_south, has_north = i > 0, i < n_lat - 1
    left = lax.rem(j + n_lev - 1, n_lev)

    barrier = pltpu.get_barrier_semaphore()
    for d in range(1, n_lev):
        pl.semaphore_signal(barrier, inc=1, device_id=(i, lax.rem(j + d, n_lev)), device_id_type=MESH)

    @pl.when(has_south)
    def _():
        pl.semaphore_signal(barrier, inc=1, device_id=(i - 1, j), device_id_type=MESH)

    @pl.when(has_north)
    def _():
        pl.semaphore_signal(barrier, inc=1, device_id=(i + 1, j), device_id_type=MESH)

    small = [
        pltpu.make_async_copy(src, dst, load_sem.at[number])
        for number, (src, dst) in enumerate((
            (span_hbm, span_s), (temp_hbm, temp_v), (mc_hbm, mc_v), (zc_hbm, zc_v),
            (fall_hbm, fall_s), (rate_hbm, rate_v)))
    ]
    big = [[pltpu.make_async_copy(q_hbm.at[:, r, k, :], q_v.at[r, k], q_sem.at[r * levels + k])
            for k in range(levels)] for r in range(rows)]
    for load in small[:4]:
        load.start()
    order = list(dict.fromkeys(
        n for pair in pairs for r in pair for n in (r - 1, r, r + 1) if 0 <= n < rows))
    for r in order:
        for load in big[r]:
            load.start()
    for load in small[4:]:
        load.start()

    def main_copy(m, ch):
        return pltpu.make_async_remote_copy(
            main_s.at[m, ch], main_r.at[j, ch], main_ss.at[m, ch], main_rs.at[j, ch], (i, m), MESH)

    def main_arrival(m, ch):
        return pltpu.make_async_remote_copy(
            main_s.at[m, ch], main_r.at[m, ch], main_ss.at[m, ch], main_rs.at[m, ch], (i, m), MESH)

    def thick_copy(m):
        return pltpu.make_async_remote_copy(
            thick_s.at[m], thick_r.at[j], thick_ss.at[m], thick_rs.at[j], (i, m), MESH)

    def below_copy(m):
        return pltpu.make_async_remote_copy(
            below_s.at[m], below_r.at[j], below_ss.at[m], below_rs.at[j], (i, m), MESH)

    north_copies = [
        pltpu.make_async_remote_copy(
            q_hbm.at[:, rows - 1, k, :], south_r.at[k], north_ss.at[k], north_rs.at[k], (i + 1, j), MESH)
        for k in range(levels)]
    south_copies = [
        pltpu.make_async_remote_copy(
            q_hbm.at[:, 0, k, :], north_r.at[k], south_ss.at[k], south_rs.at[k], (i - 1, j), MESH)
        for k in range(levels)]
    south_copies.append(pltpu.make_async_remote_copy(
        mc_hbm.at[0], mcn_r, south_ss.at[levels], south_rs.at[levels], (i - 1, j), MESH))
    halo_copy = pltpu.make_async_remote_copy(
        halo_s, halo_r, halo_sem.at[0], halo_sem.at[1], (i, left), MESH)

    lane = lax.broadcasted_iota(jnp.int32, (TILE, LANES), 1)
    sub = lax.broadcasted_iota(jnp.int32, (TILE, LANES), 0)
    spare = (lane > width) & (lane <= width + piece)
    upper = sub < TILE // 2
    first = (lane < piece - 1) | (lane == LANES - 1)
    second = lane < 2 * piece - 1

    def there(x, p):
        return pltpu.roll(x, (width + 2 - piece * p) % LANES, 1)

    def back(x, p):
        return pltpu.roll(x, (piece * p - width - 2) % LANES, 1)

    def twelve(a, b):
        turned = pltpu.roll(b, TILE // 2, 0)
        a = jnp.where(spare, jnp.where(upper, there(turned, 0), there(b, 1)), a)
        return a, jnp.where(spare, there(turned, 2), b)[: TILE // 2]

    def sixteen(a, b):
        b = jnp.concatenate([b, b], 0)
        outer = jnp.where(first, back(a, 0), back(b, 2))
        inner = second & jnp.logical_not(first)
        return a, jnp.where(upper, b, jnp.where(inner, back(a, 1), pltpu.roll(outer, TILE // 2, 0)))

    def tiles(x):
        return [x[n * TILE : (n + 1) * TILE] for n in range(x.shape[0] // TILE)]
    zlane = lax.broadcasted_iota(jnp.int32, (deep, LANES), 1)
    base = half_way * (j // half_way)
    far = [half_way - base + n for n in range(half_way)]
    near = [base + lax.rem(j - base + n, half_way) for n in range(1, half_way)]
    waited = set()

    def lanes_of(c):
        return slice(c * LANES, min((c + 1) * LANES, total))

    def prepare(ch):
        for r in order:
            if r not in waited and any(abs(r - r2) < 2 for r2 in pairs[ch]):
                waited.add(r)
                for load in big[r]:
                    load.wait()
        for k in range(levels):
            for c in range(count):
                at = lanes_of(c)
                for side, r in enumerate(pairs[ch]):
                    x = widen(q_v[r, k, :, at])
                    south = widen(q_v[r - 1, k, :, at] if r > 0 else south_r[k, :, at])
                    north = widen(q_v[r + 1, k, :, at] if r < rows - 1 else north_r[k, :, at])
                    c_s = widen(mc_v[r, k : k + 1, at])
                    c_n = widen(mc_v[r + 1, k : k + 1, at] if r < rows - 1 else mcn_r[k : k + 1, at])
                    keep = 1.0 + jnp.minimum(c_s, 0.0) - jnp.maximum(c_n, 0.0)
                    x = keep * x + jnp.maximum(c_s, 0.0) * south - jnp.minimum(c_n, 0.0) * north
                    adv_v[ch, k, c, side * body : (side + 1) * body] = x[:body]
                    low = 2 * body + side * rest
                    adv_v[ch, k, c, low : low + rest] = x[body:]
        for m in range(n_lev):
            x, y = (tiles(lon_block(lambda c: adv_v[ch, k, c], total, width, m)) for k in range(levels))
            for n, carrier in enumerate(x[:4] + y[:2]):
                main_s[m, ch, n * TILE : (n + 1) * TILE] = jnp.where(
                    spare, there(y[2 + n // 3], n % 3), carrier)
            main_s[m, ch, base_row : base_row + TILE], main_s[m, ch, ends] = twelve(x[4], y[4])

    def send(ch):
        for m in far + near:
            main_copy(m, ch).start()
        main_r[pl.ds(j, 1), ch] = main_s[pl.ds(j, 1), ch]

    for load in small[:4]:
        load.wait()
    wide = [widen(specific_air_factor * temp_v[:, k, :] * span_s[k]) for k in range(levels)]
    for m in range(n_lev):
        x, y = (lon_block(lambda c: wide[k][:, c * LANES : (c + 1) * LANES], total, width, m)
                for k in range(levels))
        thick_s[m, :TILE], thick_s[m, TILE:] = twelve(x, y)
    zc = widen(zc_v[...])
    halo = jnp.zeros((deep, LANES), jnp.float32)
    for r in range(rows):
        halo = jnp.where(zlane == r, pltpu.roll(zc[r], r, 1) if r else zc[r], halo)
        z_v[r] = zc[r]
    halo_s[...] = halo
    prepare(0)

    pl.semaphore_wait(barrier, n_lev - 1 + jnp.minimum(i, 1) + jnp.minimum(n_lat - 1 - i, 1))
    @pl.when(has_south)
    def _():
        for copy in south_copies:
            copy.start()

    for m in far + near:
        thick_copy(m).start()
    halo_copy.start()
    for m in far:
        main_copy(m, 0).start()

    @pl.when(has_north)
    def _():
        for copy in north_copies:
            copy.start()

    for m in near:
        main_copy(m, 0).start()
    main_r[pl.ds(j, 1), 0] = main_s[pl.ds(j, 1), 0]
    thick_r[pl.ds(j, 1)] = thick_s[pl.ds(j, 1)]

    prepare(1)
    send(1)

    prepare(2)
    send(2)
    for ch in range(3, len(pairs) - 1):
        prepare(ch)
        send(ch)

    for m in range(n_lev):
        @pl.when(j != m)
        def _():
            pltpu.make_async_remote_copy(
                thick_s.at[m], thick_r.at[m], thick_ss.at[m], thick_rs.at[m], (i, m), MESH).wait_recv()
    below = jnp.zeros((rows, LANES), jnp.float32)
    for m in reversed(range(n_lev)):
        below_s[m] = below
        t2 = sixteen(thick_r[m, :TILE], thick_r[m, TILE:])
        for k in reversed(range(levels)):
            t = t2[k]
            full_v[m * levels + k] = t
            dens_v[m * levels + k] = jnp.exp((below + 0.5 * t) * (-1.0 / scale_height))
            below = below + t
    for m in far + near:
        below_copy(m).start()
    below_r[pl.ds(j, 1)] = below_s[pl.ds(j, 1)]

    for load in small[4:]:
        load.wait()
    rate = rate_v[...]
    r0 = lax.broadcasted_iota(jnp.int32, rate.shape, 0)
    r1 = lax.broadcasted_iota(jnp.int32, rate.shape, 1)
    merging = jnp.where(r1 < r0, rate, jnp.where(r1 > r0, -rate, 0.0))

    def place(n):
        tail = n - 2 * body
        side = jnp.where(n < 2 * body, n // body, tail // rest)
        kind = jnp.where(n < 2 * body, n - side * body, body + tail - side * rest)
        return side, jnp.where(n < stack, kind, -1)

    _, kind = place(lax.broadcasted_iota(jnp.int32, (padded, bins), 0))
    pick = jnp.where(kind == lax.broadcasted_iota(jnp.int32, (padded, bins), 1), 1.0, 0.0)
    both = jnp.dot(pick, merging, precision=HIGHEST, preferred_element_type=jnp.float32)
    both = lax.dot_general(both, pick, (((1,), (1,)), ((), ())), precision=HIGHEST,
                           preferred_element_type=jnp.float32)
    side0, _ = place(lax.broadcasted_iota(jnp.int32, (padded, padded), 0))
    side1, _ = place(lax.broadcasted_iota(jnp.int32, (padded, padded), 1))
    both = jnp.where(side0 == side1, both, 0.0)
    high = both.astype(jnp.bfloat16)
    low = (both - high.astype(jnp.float32)).astype(jnp.bfloat16)
    merge_v[...] = jnp.concatenate([high, high, low], 1)

    def column(first, n):
        x = jnp.zeros((TILE, LANES), jnp.float32)
        for s in range(TILE):
            x = jnp.where(sub == s, fall_s[first + s % n], x)
        return x

    fall = [column(f * TILE, TILE) for f in range(full)]
    fall = jnp.concatenate(fall + fall + [column(body, rest)], 0)

    def spread(a, b):
        return jnp.concatenate([
            jnp.broadcast_to(a, (body, LANES)), jnp.broadcast_to(b, (body, LANES)),
            jnp.where(sub < rest, a, b)], 0)

    @pl.when(jnp.logical_not(has_south))
    def _():
        south_r[...] = jnp.zeros_like(south_r)

    @pl.when(jnp.logical_not(has_north))
    def _():
        north_r[...] = jnp.zeros_like(north_r)
        mcn_r[...] = jnp.zeros_like(mcn_r)

    @pl.when(has_south)
    def _():
        for k in range(levels):
            pltpu.make_async_remote_copy(
                q_hbm.at[:, 0, k, :], south_r.at[k], north_ss.at[k], north_rs.at[k], (i - 1, j), MESH).wait_recv()

    @pl.when(has_north)
    def _():
        for k in range(levels):
            pltpu.make_async_remote_copy(
                q_hbm.at[:, 0, k, :], north_r.at[k], south_ss.at[k], south_rs.at[k], (i + 1, j), MESH).wait_recv()
        pltpu.make_async_remote_copy(
            mc_hbm.at[0], mcn_r, south_ss.at[levels], south_rs.at[levels], (i + 1, j), MESH).wait_recv()

    final = len(pairs) - 1
    prepare(final)
    send(final)
    for ch, (r, r2) in enumerate(pairs):
        for k in range(deep):
            t = spread(full_v[k, r : r + 1], full_v[k, r2 : r2 + 1])
            ratio_v[ch, k] = t / (t + fall)

    halo_copy.wait_recv()
    halo = halo_r[...]
    for r in range(rows):
        z = jnp.where(zlane == width, pltpu.roll(halo, width - r, 1), z_v[r])
        up, down = jnp.maximum(z, 0.0), jnp.minimum(z, 0.0)
        z_v[r] = up
        east_v[r] = pltpu.roll(down, LANES - 1, 1)
        stay_v[r] = 1.0 + down - pltpu.roll(up, LANES - 1, 1)

    def collect(ch):
        r, r2 = pairs[ch]
        flow = jnp.zeros((stack, LANES), jnp.float32)
        last = ch == len(pairs) - 1
        for group in range(0, n_lev, 2):
            for m in (group, group + 1):
                @pl.when(j != m)
                def _():
                    main_arrival(m, ch).wait_recv()

            if last and group == n_lev - 2:
                flow_ref[...] = flow
                for m in (group, group + 1):
                    late_ref[m - group] = main_r[m, ch]
            else:
                flow = work_off(
                    width, bins, levels, group, (0, 1) if last else (r, r2),
                    [lambda at, m=m: main_r[m, ch, at] for m in (group, group + 1)], flow,
                    lambda k: ratio_v[ch, k], lambda k: read_levels(dens_v, r, r2, k),
                    lambda k: [read_rows(ref, r, r2, k) for ref in (z_v, stay_v, east_v)],
                    merge_v, pair_ref if last else out_ref)

    for ch in range(final):
        collect(ch)

    for m in range(n_lev):
        @pl.when(j != m)
        def _():
            pltpu.make_async_remote_copy(
                below_s.at[m], below_r.at[m], below_ss.at[m], below_rs.at[m], (i, m), MESH).wait_recv()
    lower = []
    for c in range(count):
        x = jnp.zeros((rows, LANES), jnp.float32)
        for m in range(n_lev):
            begin, end = m * width - c * LANES, (m + 1) * width - c * LANES
            if begin < LANES and end > 0:
                x = jnp.where((lane >= begin) & (lane < end), pltpu.roll(below_r[m], begin % LANES, 1), x)
        lower.append(x)
    below = jnp.concatenate(lower, 1)[:, :total]
    for k in reversed(range(levels)):
        t = specific_air_factor * temp_v[:, k, :] * span_s[k]
        height_ref[:, k, :] = below + 0.5 * t
        below = below + t

    halo_copy.wait_send()
    for m in far + near:
        thick_copy(m).wait_send()
        below_copy(m).wait_send()
        for ch in range(final):
            main_copy(m, ch).wait_send()

    @pl.when(has_south)
    def _():
        for copy in south_copies:
            copy.wait_send()

    @pl.when(has_north)
    def _():
        for copy in north_copies:
            copy.wait_send()

    collect(final)
    for m in far + near:
        main_copy(m, final).wait_send()


def hand_over(
    n_lev, dust_ref, height_ref, pair_ref, flow_ref, late_ref, ratio_v, dens_v, z_v, stay_v, east_v, merge_v,
    dust_out, height_out, pair_v, sem_out,
):
    bins, rows, deep, width = dust_ref.shape
    pairs = row_pairs(rows)
    leave = [pltpu.make_async_copy(dust_ref.at[:, 1 : rows - 1], dust_out.at[:, 1 : rows - 1], sem_out.at[0]),
             pltpu.make_async_copy(height_ref, height_out, sem_out.at[1])]
    for copy in leave:
        copy.start()
    r, r2 = pairs[-1]
    pair_v[...] = pair_ref[...]
    work_off(
        width, bins, deep // n_lev, n_lev - 2, (0, 1),
        [lambda at, m=m: late_ref[m, at] for m in range(2)], flow_ref[...],
        lambda k: ratio_v[len(pairs) - 1, k], lambda k: read_levels(dens_v, r, r2, k),
        lambda k: [read_rows(ref, r, r2, k) for ref in (z_v, stay_v, east_v)], merge_v, pair_v)
    for side, at in enumerate((r, r2)):
        leave.append(pltpu.make_async_copy(pair_v.at[:, side], dust_out.at[:, at], sem_out.at[2 + side]))
        leave[-1].start()
    for copy in leave:
        copy.wait()


def solution(mesh):
    n_lat, n_lev = mesh.shape["lat"], mesh.shape["lev"]
    vmem = pl.BlockSpec(memory_space=pltpu.VMEM)
    hbm = pl.BlockSpec(memory_space=pltpu.HBM)

    def on_device(*args):
        bins, rows, levels, total = args[0].shape
        width = total // n_lev
        full, rest = bins // 8, bins % 8
        assert full == 2 and rest == 4 and rows == 8 and levels == 2 and n_lev % 2 == 0
        assert width + 1 + -(-(width + 2) // 3) < LANES
        deep = n_lev * levels
        count = -(-total // LANES)
        chunks = len(row_pairs(rows))
        stack = 2 * bins
        padded = -(-stack // 16) * 16
        f32 = jnp.float32
        main = pltpu.VMEM((n_lev, chunks, 7 * TILE + TILE // 2, LANES), f32)
        thick = pltpu.VMEM((n_lev, rows + TILE // 2, LANES), f32)
        edge = pltpu.VMEM((levels, bins, total), f32)
        tile = pltpu.VMEM((n_lev, rows, LANES), f32)
        halo = pltpu.VMEM((deep, LANES), f32)
        dma = pltpu.SemaphoreType.DMA
        args = [pltpu.with_memory_space_constraint(x, pltpu.HBM) for x in args]
        outcome = pl.pallas_call(
            functools.partial(kernel, n_lat, n_lev),
            out_shape=(
                pltpu.VMEM((bins, rows, deep, width), f32),
                pltpu.VMEM((rows, levels, total), f32),
                pltpu.VMEM((bins, 2, deep, width), f32),
                pltpu.VMEM((stack, LANES), f32),
                pltpu.VMEM((2, 7 * TILE + TILE // 2, LANES), f32),
                pltpu.VMEM((chunks, deep, stack, LANES), f32),
                pltpu.VMEM((deep, rows, LANES), f32),
                pltpu.VMEM((rows, deep, LANES), f32),
                pltpu.VMEM((rows, deep, LANES), f32),
                pltpu.VMEM((rows, deep, LANES), f32),
                pltpu.VMEM((padded, 3 * padded), jnp.bfloat16),
            ),
            in_specs=[hbm] * 7,
            out_specs=(vmem,) * 11,
            scratch_shapes=[
                pltpu.VMEM((rows, levels, bins, total), f32),
                pltpu.VMEM((rows, levels, total), f32), pltpu.VMEM((rows, levels, total), f32),
                pltpu.SMEM((levels,), f32), pltpu.SMEM((bins,), f32),
                pltpu.VMEM((rows, deep, width), f32), pltpu.VMEM((bins, bins), f32),
                main, main, thick, thick, edge, edge, pltpu.VMEM((levels, total), f32), tile, tile,
                halo, halo,
                pltpu.VMEM((chunks, levels, count, stack, LANES), f32),
                pltpu.VMEM((deep, rows, LANES), f32),
                dma((rows * levels,)), dma((6,)),
                dma((n_lev, chunks)), dma((n_lev, chunks)),
                dma((n_lev,)), dma((n_lev,)), dma((n_lev,)), dma((n_lev,)),
                dma((levels,)), dma((levels,)), dma((levels + 1,)), dma((levels + 1,)), dma((2,)),
            ],
            compiler_params=pltpu.CompilerParams(
                collective_id=0, has_side_effects=True, vmem_limit_bytes=32 * 1024 * 1024),
        )(*args)
        return pl.pallas_call(
            functools.partial(hand_over, n_lev),
            out_shape=(
                jax.ShapeDtypeStruct((bins, rows, deep, width), f32),
                jax.ShapeDtypeStruct((rows, levels, total), f32)),
            in_specs=[vmem] * 11,
            out_specs=(hbm, hbm),
            scratch_shapes=[pltpu.VMEM((bins, 2, deep, width), f32), dma((4,))],
            compiler_params=pltpu.CompilerParams(vmem_limit_bytes=32 * 1024 * 1024),
        )(*outcome)

    in_specs = (
        P(None, "lat", "lev", None),
        P("lat", "lev", None),
        P("lat", "lev", None),
        P("lev"),
        P(),
        P("lat", None, "lev"),
        P(),
    )
    out_specs = (P(None, "lat", None, "lev"), P("lat", "lev", None))
    return jax.shard_map(
        on_device, mesh=mesh, in_specs=in_specs, out_specs=out_specs, check_vma=False
    )
```
